128 devices in a mesh: dp: 8 (over x, z_lo), tensor: 16 (over y, z_hi, core).
Axes of the slice: x: 4, y: 4, z: 4 (z_hi: 2, z_lo: 2; z = z_hi * 2 + z_lo), core: 2. Of those that a mesh axis runs over, the one named last changes fastest.
Arguments:
- tokens: bfloat16 [1024, 8192], P('dp', 'tensor'), may hold values from -6 to 6
- gate_weight: bfloat16 [8192, 16384], P(('dp', 'tensor')), may hold values from -0.0625 to 0.0625
- up_weight: bfloat16 [8192, 16384], P(('dp', 'tensor')), may hold values from -0.0625 to 0.0625
- gate_tangent: bfloat16 [8192, 16384], P(('dp', 'tensor')), may hold values from -0.0625 to 0.0625
- up_tangent: bfloat16 [8192, 16384], P(('dp', 'tensor')), may hold values from -0.0625 to 0.0625
- adjoint: bfloat16 [1024, 16384], P(None, ('dp', 'tensor')), may hold values from -0.1875 to 0.1875
Outputs:
- hvp_gate: float32 [8192, 16384], P(None, ('dp', 'tensor'))
- hvp_up: float32 [8192, 16384], P(None, ('dp', 'tensor'))
The draws below stay inside these ranges and needn't reach their ends.
All inputs are finite; a program needn't handle non-finite values.
Results may differ from the reference program's by a relative error of at most 0.0055.
Values may be sent and summed in bfloat16 or wider, within the bound.
A program may use at most 192 MiB of HBM per device.

```python
import jax
import jax.numpy as jnp
from jax import lax

D = 8192
FF = 16384
TOKENS = 1024


def block_levels(rng, shape, pieces, least, high):
    def one(dim, parts):
        steps = jax.random.uniform(jax.random.fold_in(jax.random.fold_in(rng, 6), dim), (parts,), jnp.float32, least / len(pieces), high / len(pieces))
        return jnp.repeat(jnp.exp(steps), shape[dim] // parts).reshape((-1,) + (1,) * (len(shape) - dim - 1))

    factor_of = one(*pieces[0])
    for cut in pieces[1:]:
        factor_of = factor_of * one(*cut)
    return factor_of


def normal_values(stream_key, dims, spread, bound, cuts=(), held_as=jnp.bfloat16):
    entries = jax.random.normal(stream_key, dims, jnp.float32) * spread
    if len(cuts) > 0:
        entries = block_levels(stream_key, dims, cuts, -0.22, 0.18) * entries
    return jnp.clip(entries, min=-bound, max=bound).astype(held_as)


def setup_inputs(seed: int = 0) -> dict:
    key_of = jax.random.split(jax.random.key(seed), 7)
    tokens = normal_values(key_of[0], (TOKENS, D), 1.0, 6.0, ((0, 8), (1, 16)))
    gate_weight = normal_values(key_of[1], (D, FF), D ** -0.5, 0.0625, ((0, 128),))
    up_weight = normal_values(key_of[2], (D, FF), D ** -0.5, 0.0625, ((0, 128),))
    gate_tangent = normal_values(key_of[3], (D, FF), D ** -0.5, 0.0625, ((0, 128),))
    up_tangent = normal_values(key_of[4], (D, FF), D ** -0.5, 0.0625, ((0, 128),))
    adjoint = normal_values(key_of[5], (TOKENS, FF), TOKENS ** -0.5, 0.1875, ((1, 128),))
    return dict(tokens=tokens, gate_weight=gate_weight, up_weight=up_weight, gate_tangent=gate_tangent, up_tangent=up_tangent, adjoint=adjoint)


def reference(tokens, gate_weight, up_weight, gate_tangent, up_tangent, adjoint):
    wide = tokens.astype(jnp.float32)
    variance = lax.optimization_barrier(jnp.mean(wide * wide, axis=1, keepdims=True)) + 1e-05
    normed = (wide * lax.rsqrt(variance)).astype(jnp.bfloat16)
    gate_pre = jnp.dot(normed, gate_weight, preferred_element_type=jnp.float32)
    up_pre = jnp.dot(normed, up_weight, preferred_element_type=jnp.float32)
    gate_dot = jnp.dot(normed, gate_tangent, preferred_element_type=jnp.float32)
    up_dot = jnp.dot(normed, up_tangent, preferred_element_type=jnp.float32)
    cotangent = adjoint.astype(jnp.float32)
    logistic = jax.nn.sigmoid(gate_pre)
    first = logistic * (1.0 + gate_pre * (1.0 - logistic))
    second = logistic * (1.0 - logistic) * (2.0 + gate_pre * (1.0 - 2.0 * logistic))
    gate_term = (cotangent * (up_dot * first + up_pre * second * gate_dot)).astype(jnp.bfloat16)
    up_term = (cotangent * first * gate_dot).astype(jnp.bfloat16)
    hvp_gate = jnp.dot(normed.T, gate_term, preferred_element_type=jnp.float32)
    hvp_up = jnp.dot(normed.T, up_term, preferred_element_type=jnp.float32)
    return (hvp_gate, hvp_up)
```

```python
import jax
import jax.numpy as jnp
from jax import lax
from jax.experimental import pallas as pl
from jax.experimental.pallas import tpu as pltpu
from jax.sharding import PartitionSpec as P

epsilon = 1e-05
MESH = pl.DeviceIdType.MESH
BF16, F32 = jnp.bfloat16, jnp.float32
PLANE = (
    (1, 0), (0, 1), (3, 0), (0, 3), (2, 0), (0, 2), (1, 1), (3, 3),
    (1, 3), (3, 1), (1, 2), (2, 1), (3, 2), (2, 3), (2, 2),
)
WAVES = (2, 1, 3, 0)


def place():
    dp, t = lax.axis_index("dp"), lax.axis_index("tensor")
    return dp // 2, t // 4, ((t // 2) % 2) * 2 + dp % 2, t % 2


def device(x, y, z, c):
    return (x * 2 + z % 2, (y * 2 + z // 2) * 2 + c)


def chip_in_plane(y, z):
    return (z % 2) * 8 + y * 2 + z // 2


def hidden_terms(forward, adjoint):
    gate_pre, up_pre = forward[:, :128], forward[:, 128:256]
    gate_dot, up_dot = forward[:, 256:384], forward[:, 384:]
    cotangent = adjoint.astype(F32)
    logistic = jax.nn.sigmoid(gate_pre)
    first = logistic * (1.0 + gate_pre * (1.0 - logistic))
    second = logistic * (1.0 - logistic) * (2.0 + gate_pre * (1.0 - 2.0 * logistic))
    gate_term = (cotangent * (up_dot * first + up_pre * second * gate_dot)).astype(BF16)
    up_term = (cotangent * first * gate_dot).astype(BF16)
    return gate_term, up_term


def exchange(
    tokens, adjoint, w0, w1, w2, w3, gathered, terms,
    staged, theirs, packed, arrived, stats, own, slab_t, slab, sums, sent, got,
    stage_sem, their_send, their_recv, wave_send, wave_recv, stat_sem, local_sem,
    y_sem, z_sem, x_send, x_left, x_right, f_send, f_left, f_right, d_send, d_recv, p_send, p_recv,
):
    weights = (w0, w1, w2, w3)
    x, y, z, c = place()
    me = chip_in_plane(y, z)
    right, left, across = (x + 1) % 4, (x + 3) % 4, (x + 2) % 4
    partner = device(x, y, z, 1 - c)

    def stage_copies(w):
        start = pl.multiple_of(((x + WAVES[w]) % 4) * 4096, 4096)
        return [
            pltpu.make_async_copy(
                weights[m].at[:, pl.ds(start, 4096)], staged.at[w % 2, m], stage_sem.at[w % 2, m]
            )
            for m in range(4)
        ]

    def stage(w):
        for copy in stage_copies(w):
            copy.start()

    def their_copy(w):
        return pltpu.make_async_remote_copy(
            theirs.at[w % 2],
            packed.at[w, :, :, pl.ds(pl.multiple_of(c * 64, 64), 64), :],
            their_send.at[w % 2],
            their_recv.at[w],
            partner,
            MESH,
        )

    def pack(w):
        for copy in stage_copies(w):
            copy.wait()
        if w >= 2:
            their_copy(w - 2).wait_send()

        @pl.loop(0, 16)
        def _(q):
            for m in range(4):
                both = staged[w % 2, m, :, pl.ds(pl.multiple_of(q * 256, 256), 256)]
                low, high = both[:, :128], both[:, 128:]
                packed[w, q, m, pl.ds(pl.multiple_of(c * 64, 64), 64), :] = jnp.where(c == 0, low, high)
                theirs[w % 2, q, m] = jnp.where(c == 0, high, low)

        their_copy(w).start()
        if w + 2 < 4:
            stage(w + 2)

    def send_wave(w):
        their_copy(w).wait_recv()
        for dy, dz in PLANE:
            to_y, to_z = (y + dy) % 4, (z + dz) % 4
            pltpu.make_async_remote_copy(
                packed.at[w, chip_in_plane(to_y, to_z)],
                arrived.at[w, me],
                wave_send.at[w],
                wave_recv.at[w],
                device(x, to_y, to_z, c),
                MESH,
            ).start()
        pltpu.make_async_copy(packed.at[w, me], arrived.at[w, me], wave_recv.at[w]).start()

    def wait_bytes(ref, sem):
        pltpu.make_async_copy(ref, ref, sem).wait()

    def partial_copy(w):
        return pltpu.make_async_remote_copy(
            sent.at[w], got.at[w], p_send.at[w], p_recv.at[w],
            device((x + WAVES[w]) % 4, y, z, c), MESH,
        )

    def share(block, which):
        pltpu.make_async_remote_copy(block, block, d_send, d_recv.at[which], partner, MESH).start()

    to_right, to_left = device(right, y, z, c), device(left, y, z, c)
    right_order = [(x + 2) % 4, (x + 1) % 4, (x + 3) % 4, x]
    left_order = [(x + 2) % 4, (x + 3) % 4, (x + 1) % 4, x]

    def send_group(i):
        block = gathered.at[x, right_order[i], c]
        pltpu.make_async_remote_copy(block, block, x_send, x_left.at[i], to_right, MESH).start()
        block = gathered.at[x, left_order[i], c]
        pltpu.make_async_remote_copy(block, block, x_send, x_right.at[i], to_left, MESH).start()

    from_left = [(x + 1) % 4, x, (x + 2) % 4, (x + 3) % 4]
    from_right = [(x + 3) % 4, x, (x + 2) % 4, (x + 1) % 4]

    def pass_on(i):
        wait_bytes(gathered.at[left, from_left[i], c], x_left.at[i])
        half = gathered.at[left, from_left[i], c, pl.ds(0, 2)]
        pltpu.make_async_remote_copy(half, half, f_send, f_left.at[i], to_right, MESH).start()
        wait_bytes(gathered.at[right, from_right[i], c], x_right.at[i])
        half = gathered.at[right, from_right[i], c, pl.ds(2, 2)]
        pltpu.make_async_remote_copy(half, half, f_send, f_right.at[i], to_left, MESH).start()
        share(gathered.at[left, from_left[i], c], 0 if i == 1 else 1)
        share(gathered.at[right, from_right[i], c], 0 if i == 1 else 1)

    across_left = [x, (x + 3) % 4, (x + 1) % 4, (x + 2) % 4]
    across_right = [x, (x + 1) % 4, (x + 3) % 4, (x + 2) % 4]

    def take_across(i):
        half = gathered.at[across, across_left[i], c, pl.ds(0, 2)]
        wait_bytes(half, f_left.at[i])
        share(half, 0 if i == 0 else 1)
        half = gathered.at[across, across_right[i], c, pl.ds(2, 2)]
        wait_bytes(half, f_right.at[i])
        share(half, 0 if i == 0 else 1)

    def forward(w):
        wait_bytes(arrived.at[w], wave_recv.at[w])
        if w + 2 < 4:
            send_wave(w + 2)

        @pl.loop(0, 2)
        def _(half):
            rows = pl.ds(pl.multiple_of(half * 512, 512), 512)
            lhs = jnp.concatenate([slab[k, rows, :] for k in range(4)], axis=1)
            rhs = jnp.concatenate([arrived[w, :, m].reshape(2048, 128) for m in range(4)], axis=1)
            total = jnp.dot(lhs, rhs, preferred_element_type=F32)
            if w < 3:
                sent[w, rows, :] = total.astype(BF16)
            else:
                sums[rows, :] = total

        if w < 3:
            partial_copy(w).start()

    stage(0)
    stage(1)
    barrier = pltpu.get_barrier_semaphore()
    peers = [device(x, (y + dy) % 4, (z + dz) % 4, c) for dy, dz in PLANE]
    stat_peers = [
        device(x, (y + dy) % 4, (z + dz) % 4, (c + dc) % 2)
        for dy in range(4) for dz in (0, 2) for dc in range(2) if dy or dz or dc
    ]
    cross_peers = [
        device(x, (y + dy) % 4, (z + dz) % 4, 1 - c) for dy in range(4) for dz in (0, 2)
    ]
    x_peers = [device((x + d) % 4, y, z, c) for d in (1, 2, 3)]
    everyone = peers + cross_peers + x_peers
    for peer in everyone:
        pl.semaphore_signal(barrier, 1, device_id=peer, device_id_type=MESH)

    wide = jnp.transpose(tokens[...].astype(F32))
    t = lax.axis_index("tensor")
    stats[t] = jnp.broadcast_to(jnp.sum(wide * wide, axis=0, keepdims=True), (8, 128))
    pl.semaphore_wait(barrier, len(everyone))
    for peer in stat_peers:
        pltpu.make_async_remote_copy(
            stats.at[t], stats.at[t], stat_sem.at[0], stat_sem.at[1], peer, MESH
        ).start()
    pack(0)
    wait_bytes(stats.at[pl.ds(0, 15)], stat_sem.at[1])
    total = stats[0]
    for i in range(1, 16):
        total = total + stats[i]
    scale = lax.rsqrt(total[:1] * (1.0 / 8192.0) + epsilon)
    wide = jnp.transpose(tokens[...].astype(F32))
    own[...] = (wide * scale).astype(BF16)
    mine = gathered.at[x, y, c, z]
    for d in (1, 3, 2):
        pltpu.make_async_remote_copy(
            own, mine, y_sem.at[0], y_sem.at[1], device(x, (y + d) % 4, z, c), MESH
        ).start()
    local = pltpu.make_async_copy(own, mine, local_sem)
    local.start()
    send_wave(0)
    pack(1)
    local.wait()
    wait_bytes(gathered.at[x, pl.ds(0, 3), c, z], y_sem.at[1])
    column = gathered.at[x, :, c, z]
    for d in (1, 3, 2):
        pltpu.make_async_remote_copy(
            column, column, z_sem.at[0], z_sem.at[1], device(x, y, (z + d) % 4, c), MESH
        ).start()
    send_wave(1)
    pack(2)
    wait_bytes(gathered.at[x, pl.ds(0, 3), c], z_sem.at[1])
    send_group(0)
    send_group(1)
    share(gathered.at[x, x, c], 0)
    for d in (1, 2, 3):
        share(gathered.at[x, (x + d) % 4, c], 1)
    pack(3)
    pass_on(0)
    send_group(2)
    pass_on(1)
    send_group(3)
    take_across(0)
    wait_bytes(gathered.at[:, x, 1 - c], d_recv.at[0])
    load = pltpu.make_async_copy(gathered.at[:, x], slab_t, local_sem)
    load.start()
    load.wait()

    @pl.loop(0, 4)
    def _(from_x):
        for from_c in range(2):
            for from_z in range(4):
                dp = from_x * 2 + from_z % 2
                rows = pl.ds(pl.multiple_of(dp * 128, 128), 128)
                slab[(from_z // 2) * 2 + from_c, rows, :] = jnp.transpose(slab_t[from_x, from_c, from_z])

    forward(0)
    pass_on(2)
    forward(1)
    pass_on(3)
    take_across(1)
    forward(2)
    take_across(2)
    take_across(3)
    forward(3)
    for w in range(3):
        partial_copy(w).wait_recv()

    @pl.loop(0, 4)
    def _(part):
        rows = pl.ds(pl.multiple_of(part * 256, 256), 256)
        total = sums[rows, :]
        for w in range(3):
            total = total + got[w, rows, :].astype(F32)
        gate_term, up_term = hidden_terms(total, adjoint[rows, :])
        terms[rows, :128] = gate_term
        terms[rows, 128:] = up_term

    wait_bytes(gathered.at[pl.ds(0, 3), pl.ds(0, 2)], d_recv.at[1])
    for w in range(3):
        partial_copy(w).wait_send()
    for w in range(4):
        wait_bytes(packed.at[w, pl.ds(0, 15)], wave_send.at[w])
    for w in (2, 3):
        their_copy(w).wait_send()
    wait_bytes(stats.at[pl.ds(0, 15)], stat_sem.at[0])
    wait_bytes(gathered.at[0, 0, 0, pl.ds(0, 3)], y_sem.at[0])
    wait_bytes(gathered.at[0, pl.ds(0, 3), 0], z_sem.at[0])
    wait_bytes(gathered.at[0], x_send)
    wait_bytes(gathered.at[0, pl.ds(0, 2)], f_send)
    wait_bytes(gathered.at[pl.ds(0, 2)], d_send)


def product(blocks, terms, gate, up):
    lhs = jnp.concatenate([blocks[i, 0, 0, j] for i in range(4) for j in range(2)], axis=1)
    result = jnp.dot(lhs, terms[...], preferred_element_type=F32)
    gate[...] = result[:, :128]
    up[...] = result[:, 128:]


def local(tokens, gate_weight, up_weight, gate_tangent, up_tangent, adjoint):
    dma = pltpu.SemaphoreType.DMA
    gathered, terms = pl.pallas_call(
        exchange,
        out_shape=(
            jax.ShapeDtypeStruct((4, 4, 2, 4, 512, 128), BF16),
            jax.ShapeDtypeStruct((1024, 256), BF16),
        ),
        in_specs=[pl.BlockSpec(memory_space=pltpu.VMEM)] * 2 + [pl.BlockSpec(memory_space=pl.ANY)] * 4,
        out_specs=(pl.BlockSpec(memory_space=pl.ANY), pl.BlockSpec(memory_space=pltpu.VMEM)),
        scratch_shapes=[
            pltpu.VMEM((2, 4, 64, 4096), BF16),
            pltpu.VMEM((2, 16, 4, 64, 128), BF16),
            pltpu.VMEM((4, 16, 4, 128, 128), BF16),
            pltpu.VMEM((4, 16, 4, 128, 128), BF16),
            pltpu.VMEM((16, 8, 128), F32),
            pltpu.VMEM((512, 128), BF16),
            pltpu.VMEM((4, 2, 4, 512, 128), BF16),
            pltpu.VMEM((4, 1024, 512), BF16),
            pltpu.VMEM((1024, 512), F32),
            pltpu.VMEM((3, 1024, 512), BF16),
            pltpu.VMEM((3, 1024, 512), BF16),
            dma((2, 4)), dma((2,)), dma((4,)), dma((4,)), dma((4,)), dma((2,)), dma,
            dma((2,)), dma((2,)), dma, dma((4,)), dma((4,)), dma, dma((4,)), dma((4,)),
            dma, dma((2,)), dma((3,)), dma((3,)),
        ],
        compiler_params=pltpu.CompilerParams(
            collective_id=0, has_side_effects=True, vmem_limit_bytes=58 * 2**20
        ),
        name="exchange",
    )(tokens, adjoint, gate_weight, up_weight, gate_tangent, up_tangent)

    return pl.pallas_call(
        product,
        grid=(16,),
        out_shape=(jax.ShapeDtypeStruct((8192, 128), F32),) * 2,
        in_specs=[
            pl.BlockSpec((4, 1, 1, 2, 512, 128), lambda t: (0, t // 4, t % 2, (t // 2) % 2, 0, 0)),
            pl.BlockSpec((1024, 256), lambda t: (0, 0)),
        ],
        out_specs=(pl.BlockSpec((512, 128), lambda t: (t, 0)),) * 2,
        compiler_params=pltpu.CompilerParams(vmem_limit_bytes=58 * 2**20),
        name="product",
    )(gathered, terms)


def solution(mesh):
    in_specs = (
        P("dp", "tensor"),
        P(("dp", "tensor"), None),
        P(("dp", "tensor"), None),
        P(("dp", "tensor"), None),
        P(("dp", "tensor"), None),
        P(None, ("dp", "tensor")),
    )
    out_specs = (P(None, ("dp", "tensor")), P(None, ("dp", "tensor")))
    return jax.shard_map(local, mesh=mesh, in_specs=in_specs, out_specs=out_specs, check_vma=False)
```

```python
import jax
import jax.numpy as jnp
from jax import lax
from jax.experimental import pallas as pl
from jax.experimental.pallas import tpu as pltpu
from jax.sharding import PartitionSpec as P

epsilon = 1e-05
MESH = pl.DeviceIdType.MESH
BF16, F32 = jnp.bfloat16, jnp.float32
PLANE = (
    (1, 0), (0, 1), (3, 0), (0, 3), (2, 0), (0, 2), (1, 1), (3, 3),
    (1, 3), (3, 1), (1, 2), (2, 1), (3, 2), (2, 3), (2, 2),
)
WAVES = (2, 1, 3, 0)


def place():
    dp, t = lax.axis_index("dp"), lax.axis_index("tensor")
    return dp // 2, t // 4, ((t // 2) % 2) * 2 + dp % 2, t % 2


def device(x, y, z, c):
    return (x * 2 + z % 2, (y * 2 + z // 2) * 2 + c)


def chip_in_plane(y, z):
    return (z % 2) * 8 + y * 2 + z // 2


def hidden_terms(forward, adjoint):
    gate_pre, up_pre = forward[:, :128], forward[:, 128:256]
    gate_dot, up_dot = forward[:, 256:384], forward[:, 384:]
    cotangent = adjoint.astype(F32)
    logistic = jax.nn.sigmoid(gate_pre)
    first = logistic * (1.0 + gate_pre * (1.0 - logistic))
    second = logistic * (1.0 - logistic) * (2.0 + gate_pre * (1.0 - 2.0 * logistic))
    gate_term = (cotangent * (up_dot * first + up_pre * second * gate_dot)).astype(BF16)
    up_term = (cotangent * first * gate_dot).astype(BF16)
    return gate_term, up_term


def exchange(
    tokens, adjoint, w0, w1, w2, w3, gathered, terms,
    staged, theirs, packed, arrived, stats, own, slab_t, slab, sums, held, sent, passing, got,
    stage_sem, their_send, their_recv, wave_send, wave_recv, stat_sem, local_sem,
    a_sem, b_send, b_recv, x_send, x_left, x_right, f_send, f_left, f_right, d_send, d_recv,
    pass_send, pass_recv, p_send, p_recv,
):
    weights = (w0, w1, w2, w3)
    x, y, z, c = place()
    me = chip_in_plane(y, z)
    right, left, across = (x + 1) % 4, (x + 3) % 4, (x + 2) % 4
    partner = device(x, y, z, 1 - c)
    to_right, to_left = device(right, y, z, c), device(left, y, z, c)
    a, b = y * (1 - c) + z * c, z * (1 - c) + y * c

    def at_ab(to_a, to_b):
        return device(x, to_a * (1 - c) + to_b * c, to_b * (1 - c) + to_a * c, c)

    def stage_copies(w):
        start = pl.multiple_of(((x + WAVES[w]) % 4) * 4096, 4096)
        return [
            pltpu.make_async_copy(
                weights[m].at[:, pl.ds(start, 4096)], staged.at[w % 2, m], stage_sem.at[w % 2, m]
            )
            for m in range(4)
        ]

    def stage(w):
        for copy in stage_copies(w):
            copy.start()

    def their_copy(w):
        return pltpu.make_async_remote_copy(
            theirs.at[w % 2],
            packed.at[w, :, :, pl.ds(pl.multiple_of(c * 64, 64), 64), :],
            their_send.at[w % 2],
            their_recv.at[w],
            partner,
            MESH,
        )

    def pack(w):
        for copy in stage_copies(w):
            copy.wait()
        if w >= 2:
            their_copy(w - 2).wait_send()

        @pl.loop(0, 16)
        def _(q):
            for m in range(4):
                both = staged[w % 2, m, :, pl.ds(pl.multiple_of(q * 256, 256), 256)]
                low, high = both[:, :128], both[:, 128:]
                packed[w, q, m, pl.ds(pl.multiple_of(c * 64, 64), 64), :] = jnp.where(c == 0, low, high)
                theirs[w % 2, q, m] = jnp.where(c == 0, high, low)

        their_copy(w).start()
        if w + 2 < 4:
            stage(w + 2)

    def send_wave(w):
        their_copy(w).wait_recv()
        for dy, dz in PLANE:
            to_y, to_z = (y + dy) % 4, (z + dz) % 4
            pltpu.make_async_remote_copy(
                packed.at[w, chip_in_plane(to_y, to_z)],
                arrived.at[w, me],
                wave_send.at[w],
                wave_recv.at[w],
                device(x, to_y, to_z, c),
                MESH,
            ).start()
        pltpu.make_async_copy(packed.at[w, me], arrived.at[w, me], wave_recv.at[w]).start()

    def wait_bytes(ref, sem):
        pltpu.make_async_copy(ref, ref, sem).wait()

    def share(block):
        pltpu.make_async_remote_copy(block, block, d_send, d_recv, partner, MESH).start()

    column_b = [b, (b + 3) % 4, (b + 1) % 4, (b + 2) % 4]

    def send_column(i):
        block = gathered.at[x, :, c, column_b[i]]
        if i > 0:
            wait_bytes(block, b_recv.at[i - 1])
        pltpu.make_async_remote_copy(block, block, x_send, x_left.at[i], to_right, MESH).start()
        pltpu.make_async_remote_copy(block, block, x_send, x_right.at[i], to_left, MESH).start()
        share(block)

    def pass_on(i):
        block = gathered.at[left, :, c, column_b[i]]
        wait_bytes(block, x_left.at[i])
        half = gathered.at[left, pl.ds(0, 2), c, column_b[i]]
        pltpu.make_async_remote_copy(half, half, f_send, f_left.at[i], to_right, MESH).start()
        share(block)
        block = gathered.at[right, :, c, column_b[i]]
        wait_bytes(block, x_right.at[i])
        half = gathered.at[right, pl.ds(2, 2), c, column_b[i]]
        pltpu.make_async_remote_copy(half, half, f_send, f_right.at[i], to_left, MESH).start()
        share(block)

    def take_across(i):
        wait_bytes(gathered.at[across, pl.ds(0, 2), c, column_b[i]], f_left.at[i])
        wait_bytes(gathered.at[across, pl.ds(2, 2), c, column_b[i]], f_right.at[i])
        share(gathered.at[across, :, c, column_b[i]])

    def forward(w, half):
        lhs = jnp.concatenate([slab[k, half * 512 : half * 512 + 512, :] for k in range(4)], axis=1)
        rhs = jnp.concatenate([arrived[w, :, m].reshape(2048, 128) for m in range(4)], axis=1)
        return jnp.dot(lhs, rhs, preferred_element_type=F32)

    def pass_copy(half):
        return pltpu.make_async_remote_copy(
            sent.at[0, half], passing.at[half], pass_send.at[half], pass_recv.at[half],
            to_left if half else to_right, MESH,
        )

    def partial_copy(w, half):
        return pltpu.make_async_remote_copy(
            sent.at[w, half], got.at[w - 1, half], p_send.at[w - 1, half], p_recv.at[w - 1, half],
            to_left if w == 2 else to_right, MESH,
        )

    stage(0)
    stage(1)
    barrier = pltpu.get_barrier_semaphore()
    peers = [device(x, (y + dy) % 4, (z + dz) % 4, c) for dy, dz in PLANE]
    stat_peers = [
        device(x, (y + dy) % 4, (z + dz) % 4, (c + dc) % 2)
        for dy in range(4) for dz in (0, 2) for dc in range(2) if dy or dz or dc
    ]
    cross_peers = [
        device(x, (y + dy) % 4, (z + dz) % 4, 1 - c) for dy in range(4) for dz in (0, 2)
    ]
    everyone = peers + cross_peers + [to_right, to_left]
    for peer in everyone:
        pl.semaphore_signal(barrier, 1, device_id=peer, device_id_type=MESH)

    wide = jnp.transpose(tokens[...].astype(F32))
    t = lax.axis_index("tensor")
    stats[t] = jnp.broadcast_to(jnp.sum(wide * wide, axis=0, keepdims=True), (8, 128))
    pl.semaphore_wait(barrier, len(everyone))
    for peer in stat_peers:
        pltpu.make_async_remote_copy(
            stats.at[t], stats.at[t], stat_sem.at[0], stat_sem.at[1], peer, MESH
        ).start()
    pack(0)
    wait_bytes(stats.at[pl.ds(0, 15)], stat_sem.at[1])
    total = stats[0]
    for i in range(1, 16):
        total = total + stats[i]
    scale = lax.rsqrt(total[:1] * (1.0 / 8192.0) + epsilon)
    wide = jnp.transpose(tokens[...].astype(F32))
    own[...] = (wide * scale).astype(BF16)
    mine = gathered.at[x, a, c, b]
    for d in (1, 3, 2):
        pltpu.make_async_remote_copy(
            own, mine, a_sem.at[0], a_sem.at[1], at_ab((a + d) % 4, b), MESH
        ).start()
    local = pltpu.make_async_copy(own, mine, local_sem)
    local.start()
    pack(1)
    local.wait()
    wait_bytes(gathered.at[x, pl.ds(0, 3), c, b], a_sem.at[1])
    column = gathered.at[x, :, c, b]
    for i, d in enumerate((1, 3, 2)):
        pltpu.make_async_remote_copy(
            column, column, b_send, b_recv.at[i], at_ab(a, (b + d) % 4), MESH
        ).start()
    send_column(0)
    send_wave(0)
    send_column(1)
    send_column(2)
    send_column(3)
    send_wave(1)
    pack(2)
    pass_on(0)
    send_wave(2)
    pack(3)
    pass_on(1)
    take_across(0)
    send_wave(3)
    pass_on(2)
    take_across(1)
    pass_on(3)
    take_across(2)
    take_across(3)
    wait_bytes(gathered.at[:, :, 1 - c], d_recv)
    loads = [
        pltpu.make_async_copy(gathered.at[:, x, 0], slab_t.at[0], local_sem),
        pltpu.make_async_copy(gathered.at[:, :, 1, x], slab_t.at[1], a_sem.at[1]),
    ]
    for load in loads:
        load.start()
    for load in loads:
        load.wait()

    @pl.loop(0, 4)
    def _(from_x):
        for from_c in range(2):
            for from_z in range(4):
                dp = from_x * 2 + from_z % 2
                rows = pl.ds(pl.multiple_of(dp * 128, 128), 128)
                slab[(from_z // 2) * 2 + from_c, rows, :] = jnp.transpose(slab_t[from_c, from_x, from_z])

    wait_bytes(arrived.at[0], wave_recv.at[0])
    for half in range(2):
        sent[0, half] = forward(0, half).astype(BF16)
        pass_copy(half).start()
    wait_bytes(arrived.at[1], wave_recv.at[1])
    sent[1, 1] = forward(1, 1).astype(BF16)
    partial_copy(1, 1).start()
    wait_bytes(arrived.at[2], wave_recv.at[2])
    sent[2, 0] = forward(2, 0).astype(BF16)
    partial_copy(2, 0).start()
    held[0] = forward(1, 0)
    held[1] = forward(2, 1)
    pass_copy(0).wait_recv()
    sent[1, 0] = (held[0] + passing[0].astype(F32)).astype(BF16)
    partial_copy(1, 0).start()
    pass_copy(1).wait_recv()
    sent[2, 1] = (held[1] + passing[1].astype(F32)).astype(BF16)
    partial_copy(2, 1).start()
    wait_bytes(arrived.at[3], wave_recv.at[3])
    for half in range(2):
        sums[half] = forward(3, half)

    for w, half in ((1, 1), (2, 0), (1, 0), (2, 1)):
        partial_copy(w, half).wait_recv()

    for half in range(2):
        @pl.loop(0, 2)
        def _(part):
            rows = pl.ds(pl.multiple_of(part * 256, 256), 256)
            total = sums[half, rows, :] + (got[0, half, rows, :].astype(F32) + got[1, half, rows, :].astype(F32))
            to = pl.ds(pl.multiple_of(half * 512 + part * 256, 256), 256)
            gate_term, up_term = hidden_terms(total, adjoint[to, :])
            terms[to, :128] = gate_term
            terms[to, 128:] = up_term

    for half in range(2):
        pass_copy(half).wait_send()
        for w in (1, 2):
            partial_copy(w, half).wait_send()
    for w in range(4):
        wait_bytes(packed.at[w, pl.ds(0, 15)], wave_send.at[w])
    for w in (2, 3):
        their_copy(w).wait_send()
    wait_bytes(stats.at[pl.ds(0, 15)], stat_sem.at[0])
    wait_bytes(gathered.at[0, 0, 0, pl.ds(0, 3)], a_sem.at[0])
    wait_bytes(gathered.at[0, pl.ds(0, 3), 0], b_send)
    wait_bytes(gathered.at[0], x_send)
    wait_bytes(gathered.at[0, pl.ds(0, 2)], f_send)
    wait_bytes(gathered.at[pl.ds(0, 2)], d_send)


def product(gathered, terms, gate, up, blocks, gate_out, up_out, in_sem, out_sem):
    def load(t):
        row, pair = t // 4, ((t // 2) % 2) * 2
        if t % 2 == 0:
            return pltpu.make_async_copy(
                gathered.at[:, row, 0, pl.ds(pair, 2)], blocks.at[t], in_sem.at[t]
            )
        return pltpu.make_async_copy(
            gathered.at[:, pl.ds(pair, 2), 1, row], blocks.at[t], in_sem.at[t]
        )

    def stores(t):
        rows = pl.ds(512 * t, 512)
        return (
            pltpu.make_async_copy(gate_out.at[t], gate.at[rows], out_sem.at[0, t]),
            pltpu.make_async_copy(up_out.at[t], up.at[rows], out_sem.at[1, t]),
        )

    for t in range(16):
        load(t).start()
    for t in range(16):
        load(t).wait()
        lhs = jnp.concatenate([blocks[t, i, j] for i in range(4) for j in range(2)], axis=1)
        result = jnp.dot(lhs, terms[...], preferred_element_type=F32)
        gate_out[t] = result[:, :128]
        up_out[t] = result[:, 128:]
        for store in stores(t):
            store.start()
    for t in range(16):
        for store in stores(t):
            store.wait()


def local(tokens, gate_weight, up_weight, gate_tangent, up_tangent, adjoint):
    dma = pltpu.SemaphoreType.DMA
    gathered, terms = pl.pallas_call(
        exchange,
        out_shape=(
            jax.ShapeDtypeStruct((4, 4, 2, 4, 512, 128), BF16),
            jax.ShapeDtypeStruct((1024, 256), BF16),
        ),
        in_specs=[pl.BlockSpec(memory_space=pltpu.VMEM)] * 2 + [pl.BlockSpec(memory_space=pl.ANY)] * 4,
        out_specs=(pl.BlockSpec(memory_space=pl.ANY), pl.BlockSpec(memory_space=pltpu.VMEM)),
        scratch_shapes=[
            pltpu.VMEM((2, 4, 64, 4096), BF16),
            pltpu.VMEM((2, 16, 4, 64, 128), BF16),
            pltpu.VMEM((4, 16, 4, 128, 128), BF16),
            pltpu.VMEM((4, 16, 4, 128, 128), BF16),
            pltpu.VMEM((16, 8, 128), F32),
            pltpu.VMEM((512, 128), BF16),
            pltpu.VMEM((2, 4, 4, 512, 128), BF16),
            pltpu.VMEM((4, 1024, 512), BF16),
            pltpu.VMEM((2, 512, 512), F32),
            pltpu.VMEM((2, 512, 512), F32),
            pltpu.VMEM((3, 2, 512, 512), BF16),
            pltpu.VMEM((2, 512, 512), BF16),
            pltpu.VMEM((2, 2, 512, 512), BF16),
            dma((2, 4)), dma((2,)), dma((4,)), dma((4,)), dma((4,)), dma((2,)), dma,
            dma((2,)), dma, dma((3,)), dma, dma((4,)), dma((4,)), dma, dma((4,)), dma((4,)), dma, dma,
            dma((2,)), dma((2,)), dma((2, 2)), dma((2, 2)),
        ],
        compiler_params=pltpu.CompilerParams(
            collective_id=0, has_side_effects=True, vmem_limit_bytes=58 * 2**20
        ),
        name="exchange",
    )(tokens, adjoint, gate_weight, up_weight, gate_tangent, up_tangent)

    return pl.pallas_call(
        product,
        out_shape=(jax.ShapeDtypeStruct((8192, 128), F32),) * 2,
        in_specs=[pl.BlockSpec(memory_space=pl.ANY), pl.BlockSpec(memory_space=pltpu.VMEM)],
        out_specs=(pl.BlockSpec(memory_space=pl.ANY),) * 2,
        scratch_shapes=[
            pltpu.VMEM((16, 4, 2, 512, 128), BF16),
            pltpu.VMEM((16, 512, 128), F32),
            pltpu.VMEM((16, 512, 128), F32),
            dma((16,)), dma((2, 16)),
        ],
        compiler_params=pltpu.CompilerParams(vmem_limit_bytes=58 * 2**20),
        name="product",
    )(gathered, terms)


def solution(mesh):
    in_specs = (
        P("dp", "tensor"),
        P(("dp", "tensor"), None),
        P(("dp", "tensor"), None),
        P(("dp", "tensor"), None),
        P(("dp", "tensor"), None),
        P(None, ("dp", "tensor")),
    )
    out_specs = (P(None, ("dp", "tensor")), P(None, ("dp", "tensor")))
    return jax.shard_map(local, mesh=mesh, in_specs=in_specs, out_specs=out_specs, check_vma=False)
```

```python
import jax
import jax.numpy as jnp
from jax import lax
from jax.experimental import pallas as pl
from jax.experimental.pallas import tpu as pltpu
from jax.sharding import PartitionSpec as P

epsilon = 1e-05
MESH = pl.DeviceIdType.MESH
BF16, F32 = jnp.bfloat16, jnp.float32
PLANE = (
    (1, 0), (0, 1), (3, 0), (0, 3), (2, 0), (0, 2), (1, 1), (3, 3),
    (1, 3), (3, 1), (1, 2), (2, 1), (3, 2), (2, 3), (2, 2),
)
WAVES = (2, 1, 3, 0)


def place():
    dp, t = lax.axis_index("dp"), lax.axis_index("tensor")
    return dp // 2, t // 4, ((t // 2) % 2) * 2 + dp % 2, t % 2


def device(x, y, z, c):
    return (x * 2 + z % 2, (y * 2 + z // 2) * 2 + c)


def chip_in_plane(y, z):
    return (z % 2) * 8 + y * 2 + z // 2


def hidden_terms(forward, adjoint):
    gate_pre, up_pre = forward[:, :128], forward[:, 128:256]
    gate_dot, up_dot = forward[:, 256:384], forward[:, 384:]
    cotangent = adjoint.astype(F32)
    logistic = jax.nn.sigmoid(gate_pre)
    first = logistic * (1.0 + gate_pre * (1.0 - logistic))
    second = logistic * (1.0 - logistic) * (2.0 + gate_pre * (1.0 - 2.0 * logistic))
    gate_term = (cotangent * (up_dot * first + up_pre * second * gate_dot)).astype(BF16)
    up_term = (cotangent * first * gate_dot).astype(BF16)
    return gate_term, up_term


def exchange(
    tokens, adjoint, w0, w1, w2, w3, gathered, terms,
    staged, theirs, packed, arrived, stats, own, slab_t, slab, sums, held, sent, passing, got,
    stage_sem, their_send, their_recv, wave_send, wave_recv, stat_sem, local_sem,
    a_sem, b_send, b_recv, x_send, x_left, x_right, f_send, f_left, f_right, d_send, d_recv,
    pass_send, pass_recv, p_send, p_recv,
):
    weights = (w0, w1, w2, w3)
    x, y, z, c = place()
    me = chip_in_plane(y, z)
    right, left, across = (x + 1) % 4, (x + 3) % 4, (x + 2) % 4
    partner = device(x, y, z, 1 - c)
    to_right, to_left = device(right, y, z, c), device(left, y, z, c)
    a, b = y * (1 - c) + z * c, z * (1 - c) + y * c

    def at_ab(to_a, to_b):
        return device(x, to_a * (1 - c) + to_b * c, to_b * (1 - c) + to_a * c, c)

    def stage_copies(w):
        start = pl.multiple_of(((x + WAVES[w]) % 4) * 4096, 4096)
        return [
            pltpu.make_async_copy(
                weights[m].at[:, pl.ds(start, 4096)], staged.at[w % 2, m], stage_sem.at[w % 2, m]
            )
            for m in range(4)
        ]

    def stage(w):
        for copy in stage_copies(w):
            copy.start()

    def their_copy(w):
        return pltpu.make_async_remote_copy(
            theirs.at[w % 2],
            packed.at[w, :, :, pl.ds(pl.multiple_of(c * 64, 64), 64), :],
            their_send.at[w % 2],
            their_recv.at[w],
            partner,
            MESH,
        )

    def pack(w):
        for copy in stage_copies(w):
            copy.wait()
        if w >= 2:
            their_copy(w - 2).wait_send()

        @pl.loop(0, 16)
        def _(q):
            for m in range(4):
                both = staged[w % 2, m, :, pl.ds(pl.multiple_of(q * 256, 256), 256)]
                low, high = both[:, :128], both[:, 128:]
                packed[w, q, m, pl.ds(pl.multiple_of(c * 64, 64), 64), :] = jnp.where(c == 0, low, high)
                theirs[w % 2, q, m] = jnp.where(c == 0, high, low)

        their_copy(w).start()
        if w + 2 < 4:
            stage(w + 2)

    def send_wave(w):
        their_copy(w).wait_recv()
        for dy, dz in PLANE:
            to_y, to_z = (y + dy) % 4, (z + dz) % 4
            pltpu.make_async_remote_copy(
                packed.at[w, chip_in_plane(to_y, to_z)],
                arrived.at[w, me],
                wave_send.at[w],
                wave_recv.at[w],
                device(x, to_y, to_z, c),
                MESH,
            ).start()
        pltpu.make_async_copy(packed.at[w, me], arrived.at[w, me], wave_recv.at[w]).start()

    def wait_bytes(ref, sem):
        pltpu.make_async_copy(ref, ref, sem).wait()

    def share(block):
        pltpu.make_async_remote_copy(block, block, d_send, d_recv, partner, MESH).start()

    column_b = [b, (b + 3) % 4, (b + 1) % 4, (b + 2) % 4]

    def send_column(i):
        block = gathered.at[x, :, c, column_b[i]]
        if i > 0:
            wait_bytes(block, b_recv.at[i - 1])
        pltpu.make_async_remote_copy(block, block, x_send, x_left.at[i], to_right, MESH).start()
        pltpu.make_async_remote_copy(block, block, x_send, x_right.at[i], to_left, MESH).start()
        share(block)

    def pass_on(i):
        block = gathered.at[left, :, c, column_b[i]]
        wait_bytes(block, x_left.at[i])
        half = gathered.at[left, pl.ds(0, 2), c, column_b[i]]
        pltpu.make_async_remote_copy(half, half, f_send, f_left.at[i], to_right, MESH).start()
        share(block)
        block = gathered.at[right, :, c, column_b[i]]
        wait_bytes(block, x_right.at[i])
        half = gathered.at[right, pl.ds(2, 2), c, column_b[i]]
        pltpu.make_async_remote_copy(half, half, f_send, f_right.at[i], to_left, MESH).start()
        share(block)

    def take_across(i):
        wait_bytes(gathered.at[across, pl.ds(0, 2), c, column_b[i]], f_left.at[i])
        wait_bytes(gathered.at[across, pl.ds(2, 2), c, column_b[i]], f_right.at[i])
        share(gathered.at[across, :, c, column_b[i]])

    def forward(w, half):
        lhs = jnp.concatenate([slab[k, half * 512 : half * 512 + 512, :] for k in range(4)], axis=1)
        rhs = jnp.concatenate([arrived[w, :, m].reshape(2048, 128) for m in range(4)], axis=1)
        return jnp.dot(lhs, rhs, preferred_element_type=F32)

    def pass_copy(half):
        return pltpu.make_async_remote_copy(
            sent.at[0, half], passing.at[half], pass_send.at[half], pass_recv.at[half],
            to_left if half else to_right, MESH,
        )

    def partial_copy(w, half):
        return pltpu.make_async_remote_copy(
            sent.at[w, half], got.at[w - 1, half], p_send.at[w - 1, half], p_recv.at[w - 1, half],
            to_left if w == 2 else to_right, MESH,
        )

    stage(0)
    stage(1)
    barrier = pltpu.get_barrier_semaphore()
    peers = [device(x, (y + dy) % 4, (z + dz) % 4, c) for dy, dz in PLANE]
    stat_peers = [
        device(x, (y + dy) % 4, (z + dz) % 4, (c + dc) % 2)
        for dy in range(4) for dz in (0, 2) for dc in range(2) if dy or dz or dc
    ]
    cross_peers = [
        device(x, (y + dy) % 4, (z + dz) % 4, 1 - c) for dy in range(4) for dz in (0, 2)
    ]
    everyone = peers + cross_peers + [to_right, to_left]
    for peer in everyone:
        pl.semaphore_signal(barrier, 1, device_id=peer, device_id_type=MESH)

    wide = jnp.transpose(tokens[...].astype(F32))
    t = lax.axis_index("tensor")
    stats[t] = jnp.broadcast_to(jnp.sum(wide * wide, axis=0, keepdims=True), (8, 128))
    pl.semaphore_wait(barrier, len(everyone))
    for peer in stat_peers:
        pltpu.make_async_remote_copy(
            stats.at[t], stats.at[t], stat_sem.at[0], stat_sem.at[1], peer, MESH
        ).start()
    pack(0)
    wait_bytes(stats.at[pl.ds(0, 15)], stat_sem.at[1])
    total = stats[0]
    for i in range(1, 16):
        total = total + stats[i]
    scale = lax.rsqrt(total[:1] * (1.0 / 8192.0) + epsilon)
    wide = jnp.transpose(tokens[...].astype(F32))
    own[...] = (wide * scale).astype(BF16)
    mine = gathered.at[x, a, c, b]
    for d in (1, 3, 2):
        pltpu.make_async_remote_copy(
            own, mine, a_sem.at[0], a_sem.at[1], at_ab((a + d) % 4, b), MESH
        ).start()
    local = pltpu.make_async_copy(own, mine, local_sem)
    local.start()
    pack(1)
    local.wait()
    wait_bytes(gathered.at[x, pl.ds(0, 3), c, b], a_sem.at[1])
    column = gathered.at[x, :, c, b]
    for i, d in enumerate((1, 3, 2)):
        pltpu.make_async_remote_copy(
            column, column, b_send, b_recv.at[i], at_ab(a, (b + d) % 4), MESH
        ).start()
    send_column(0)
    send_wave(0)
    send_column(1)
    send_column(2)
    send_column(3)
    send_wave(1)
    pack(2)
    pass_on(0)
    send_wave(2)
    pack(3)
    pass_on(1)
    take_across(0)
    send_wave(3)
    pass_on(2)
    take_across(1)
    pass_on(3)
    take_across(2)
    take_across(3)
    wait_bytes(gathered.at[:, :, 1 - c], d_recv)
    loads = [
        pltpu.make_async_copy(gathered.at[:, x, 0], slab_t.at[0], local_sem),
        pltpu.make_async_copy(gathered.at[:, :, 1, x], slab_t.at[1], a_sem.at[1]),
    ]
    for load in loads:
        load.start()
    for load in loads:
        load.wait()

    @pl.loop(0, 4)
    def _(from_x):
        for from_c in range(2):
            for from_z in range(4):
                dp = from_x * 2 + from_z % 2
                rows = pl.ds(pl.multiple_of(dp * 128, 128), 128)
                slab[(from_z // 2) * 2 + from_c, rows, :] = jnp.transpose(slab_t[from_c, from_x, from_z])

    wait_bytes(arrived.at[0], wave_recv.at[0])
    for half in range(2):
        sent[0, half] = forward(0, half).astype(BF16)
        pass_copy(half).start()
    wait_bytes(arrived.at[1], wave_recv.at[1])
    sent[1, 1] = forward(1, 1).astype(BF16)
    partial_copy(1, 1).start()
    wait_bytes(arrived.at[2], wave_recv.at[2])
    sent[2, 0] = forward(2, 0).astype(BF16)
    partial_copy(2, 0).start()
    held[0] = forward(1, 0)
    held[1] = forward(2, 1)
    pass_copy(0).wait_recv()
    sent[1, 0] = (held[0] + passing[0].astype(F32)).astype(BF16)
    partial_copy(1, 0).start()
    pass_copy(1).wait_recv()
    sent[2, 1] = (held[1] + passing[1].astype(F32)).astype(BF16)
    partial_copy(2, 1).start()
    wait_bytes(arrived.at[3], wave_recv.at[3])
    for half in range(2):
        sums[half] = forward(3, half)

    for w, half in ((1, 1), (2, 0), (1, 0), (2, 1)):
        partial_copy(w, half).wait_recv()

    for half in range(2):
        @pl.loop(0, 2)
        def _(part):
            rows = pl.ds(pl.multiple_of(part * 256, 256), 256)
            total = sums[half, rows, :] + (got[0, half, rows, :].astype(F32) + got[1, half, rows, :].astype(F32))
            to = pl.ds(pl.multiple_of(half * 512 + part * 256, 256), 256)
            gate_term, up_term = hidden_terms(total, adjoint[to, :])
            terms[to, :128] = gate_term
            terms[to, 128:] = up_term

    for half in range(2):
        pass_copy(half).wait_send()
        for w in (1, 2):
            partial_copy(w, half).wait_send()
    for w in range(4):
        wait_bytes(packed.at[w, pl.ds(0, 15)], wave_send.at[w])
    for w in (2, 3):
        their_copy(w).wait_send()
    wait_bytes(stats.at[pl.ds(0, 15)], stat_sem.at[0])
    wait_bytes(gathered.at[0, 0, 0, pl.ds(0, 3)], a_sem.at[0])
    wait_bytes(gathered.at[0, pl.ds(0, 3), 0], b_send)
    wait_bytes(gathered.at[0], x_send)
    wait_bytes(gathered.at[0, pl.ds(0, 2)], f_send)
    wait_bytes(gathered.at[pl.ds(0, 2)], d_send)


def product(gathered, terms, gate, up, gate_out, up_out, out_sem):
    def stores(t):
        rows = pl.ds(512 * t, 512)
        return (
            pltpu.make_async_copy(gate_out.at[t], gate.at[rows], out_sem.at[0, t]),
            pltpu.make_async_copy(up_out.at[t], up.at[rows], out_sem.at[1, t]),
        )

    for t in range(16):
        row, pair = t // 4, ((t // 2) % 2) * 2
        lhs = jnp.concatenate(
            [
                gathered[i, row, 0, pair + j] if t % 2 == 0 else gathered[i, pair + j, 1, row]
                for i in range(4)
                for j in range(2)
            ],
            axis=1,
        )
        result = jnp.dot(lhs, terms[...], preferred_element_type=F32)
        gate_out[t] = result[:, :128]
        up_out[t] = result[:, 128:]
        for store in stores(t):
            store.start()
    for t in range(16):
        for store in stores(t):
            store.wait()


def local(tokens, gate_weight, up_weight, gate_tangent, up_tangent, adjoint):
    dma = pltpu.SemaphoreType.DMA
    gathered, terms = pl.pallas_call(
        exchange,
        out_shape=(
            pltpu.VMEM((4, 4, 2, 4, 512, 128), BF16),
            pltpu.VMEM((1024, 256), BF16),
        ),
        in_specs=[pl.BlockSpec(memory_space=pltpu.VMEM)] * 2 + [pl.BlockSpec(memory_space=pl.ANY)] * 4,
        out_specs=(pl.BlockSpec(memory_space=pl.ANY), pl.BlockSpec(memory_space=pltpu.VMEM)),
        scratch_shapes=[
            pltpu.VMEM((2, 4, 64, 4096), BF16),
            pltpu.VMEM((2, 16, 4, 64, 128), BF16),
            pltpu.VMEM((4, 16, 4, 128, 128), BF16),
            pltpu.VMEM((4, 16, 4, 128, 128), BF16),
            pltpu.VMEM((16, 8, 128), F32),
            pltpu.VMEM((512, 128), BF16),
            pltpu.VMEM((2, 4, 4, 512, 128), BF16),
            pltpu.VMEM((4, 1024, 512), BF16),
            pltpu.VMEM((2, 512, 512), F32),
            pltpu.VMEM((2, 512, 512), F32),
            pltpu.VMEM((3, 2, 512, 512), BF16),
            pltpu.VMEM((2, 512, 512), BF16),
            pltpu.VMEM((2, 2, 512, 512), BF16),
            dma((2, 4)), dma((2,)), dma((4,)), dma((4,)), dma((4,)), dma((2,)), dma,
            dma((2,)), dma, dma((3,)), dma, dma((4,)), dma((4,)), dma, dma((4,)), dma((4,)), dma, dma,
            dma((2,)), dma((2,)), dma((2, 2)), dma((2, 2)),
        ],
        compiler_params=pltpu.CompilerParams(
            collective_id=0, has_side_effects=True, vmem_limit_bytes=44 * 2**20
        ),
        name="exchange",
    )(tokens, adjoint, gate_weight, up_weight, gate_tangent, up_tangent)

    gathered = pltpu.with_memory_space_constraint(gathered, pltpu.VMEM)
    terms = pltpu.with_memory_space_constraint(terms, pltpu.VMEM)
    return pl.pallas_call(
        product,
        out_shape=(jax.ShapeDtypeStruct((8192, 128), F32),) * 2,
        in_specs=[pl.BlockSpec(memory_space=pltpu.VMEM)] * 2,
        out_specs=(pl.BlockSpec(memory_space=pl.ANY),) * 2,
        scratch_shapes=[
            pltpu.VMEM((16, 512, 128), F32),
            pltpu.VMEM((16, 512, 128), F32),
            dma((2, 16)),
        ],
        compiler_params=pltpu.CompilerParams(vmem_limit_bytes=24 * 2**20),
        name="product",
    )(gathered, terms)


def solution(mesh):
    in_specs = (
        P("dp", "tensor"),
        P(("dp", "tensor"), None),
        P(("dp", "tensor"), None),
        P(("dp", "tensor"), None),
        P(("dp", "tensor"), None),
        P(None, ("dp", "tensor")),
    )
    out_specs = (P(None, ("dp", "tensor")), P(None, ("dp", "tensor")))
    return jax.shard_map(local, mesh=mesh, in_specs=in_specs, out_specs=out_specs, check_vma=False)
```

```python
import jax
import jax.numpy as jnp
from jax import lax
from jax.experimental import pallas as pl
from jax.experimental.pallas import tpu as pltpu
from jax.sharding import PartitionSpec as P

epsilon = 1e-05
MESH = pl.DeviceIdType.MESH
BF16, F32 = jnp.bfloat16, jnp.float32
PLANE = (
    (1, 0), (0, 1), (3, 0), (0, 3), (2, 0), (0, 2), (1, 1), (3, 3),
    (1, 3), (3, 1), (1, 2), (2, 1), (3, 2), (2, 3), (2, 2),
)
WAVES = (2, 1, 3, 0)


def place():
    dp, t = lax.axis_index("dp"), lax.axis_index("tensor")
    return dp // 2, t // 4, ((t // 2) % 2) * 2 + dp % 2, t % 2


def device(x, y, z, c):
    return (x * 2 + z % 2, (y * 2 + z // 2) * 2 + c)


def chip_in_plane(y, z):
    return (z % 2) * 8 + y * 2 + z // 2


def hidden_terms(forward, adjoint):
    gate_pre, up_pre = forward[:, :128], forward[:, 128:256]
    gate_dot, up_dot = forward[:, 256:384], forward[:, 384:]
    cotangent = adjoint.astype(F32)
    logistic = jax.nn.sigmoid(gate_pre)
    first = logistic * (1.0 + gate_pre * (1.0 - logistic))
    second = logistic * (1.0 - logistic) * (2.0 + gate_pre * (1.0 - 2.0 * logistic))
    gate_term = (cotangent * (up_dot * first + up_pre * second * gate_dot)).astype(BF16)
    up_term = (cotangent * first * gate_dot).astype(BF16)
    return gate_term, up_term


def exchange(
    tokens, adjoint, w0, w1, w2, w3, gathered, terms,
    staged, theirs, packed, arrived, stats, scales, slab, sums, held, sent, passing, got,
    stage_sem, their_send, their_recv, wave_send, wave_recv, stat_sem, scale_sem,
    a_send, a_recv, b_send, b_recv, x_send, x_left, x_right, f_send, f_left, f_right, d_send, d_recv,
    pass_send, pass_recv, p_send, p_recv,
):
    weights = (w0, w1, w2, w3)
    x, y, z, c = place()
    me = chip_in_plane(y, z)
    right, left, across = (x + 1) % 4, (x + 3) % 4, (x + 2) % 4
    partner = device(x, y, z, 1 - c)
    to_right, to_left = device(right, y, z, c), device(left, y, z, c)
    a, b = y * (1 - c) + z * c, z * (1 - c) + y * c

    def at_ab(to_a, to_b):
        return device(x, to_a * (1 - c) + to_b * c, to_b * (1 - c) + to_a * c, c)

    def stage_copies(w):
        start = pl.multiple_of(((x + WAVES[w]) % 4) * 4096, 4096)
        return [
            pltpu.make_async_copy(
                weights[m].at[:, pl.ds(start, 4096)], staged.at[w % 2, m], stage_sem.at[w % 2, m]
            )
            for m in range(4)
        ]

    def stage(w):
        for copy in stage_copies(w):
            copy.start()

    def their_copy(w):
        return pltpu.make_async_remote_copy(
            theirs.at[w % 2],
            packed.at[w, :, :, pl.ds(pl.multiple_of(c * 64, 64), 64), :],
            their_send.at[w % 2],
            their_recv.at[w],
            partner,
            MESH,
        )

    def pack(w):
        for copy in stage_copies(w):
            copy.wait()
        if w >= 2:
            their_copy(w - 2).wait_send()

        @pl.loop(0, 16)
        def _(q):
            for m in range(4):
                both = staged[w % 2, m, :, pl.ds(pl.multiple_of(q * 256, 256), 256)]
                low, high = both[:, :128], both[:, 128:]
                packed[w, q, m, pl.ds(pl.multiple_of(c * 64, 64), 64), :] = jnp.where(c == 0, low, high)
                theirs[w % 2, q, m] = jnp.where(c == 0, high, low)

        if w + 2 < 4:
            stage(w + 2)

    def send_wave(w):
        their_copy(w).wait_recv()
        for dy, dz in PLANE:
            to_y = (y + dy * (1 - c) + (4 - dz) * c) % 4
            to_z = (z + dz * (1 - c) + (4 - dy) * c) % 4
            pltpu.make_async_remote_copy(
                packed.at[w, chip_in_plane(to_y, to_z)],
                arrived.at[w, me],
                wave_send.at[w],
                wave_recv.at[w],
                device(x, to_y, to_z, c),
                MESH,
            ).start()
        pltpu.make_async_copy(packed.at[w, me], arrived.at[w, me], wave_recv.at[w]).start()

    def wait_bytes(ref, sem):
        pltpu.make_async_copy(ref, ref, sem).wait()

    def share(block):
        pltpu.make_async_remote_copy(block, block, d_send, d_recv, partner, MESH).start()

    column_b = [b, (b + 3) % 4, (b + 1) % 4, (b + 2) % 4]

    def send_x(i, block):
        pltpu.make_async_remote_copy(block, block, x_send, x_left.at[i], to_right, MESH).start()
        pltpu.make_async_remote_copy(block, block, x_send, x_right.at[i], to_left, MESH).start()

    def send_block(at_a):
        block = gathered.at[x, at_a, c, b]
        for i, d in enumerate((1, 3, 2)):
            pltpu.make_async_remote_copy(
                block, block, b_send, b_recv.at[i], at_ab(a, (b + d) % 4), MESH
            ).start()
        send_x(0, block)

    def send_column(i):
        block = gathered.at[x, :, c, column_b[i]]
        wait_bytes(block, b_recv.at[i - 1])
        send_x(i, block)
        share(block)

    def normalise(from_x):
        @pl.loop(0, 16)
        def _(i):
            at_a, at_b = i // 4, i % 4
            for from_c in range(2):
                from_z = at_a if from_c else at_b
                scale = scales[from_x * 2 + from_z % 2][:1]
                block = gathered[from_x, at_a, from_c, at_b].astype(F32)
                gathered[from_x, at_a, from_c, at_b] = (block * scale).astype(BF16)

    def pass_on(i):
        block = gathered.at[left, :, c, column_b[i]]
        wait_bytes(block, x_left.at[i])
        half = gathered.at[left, pl.ds(0, 2), c, column_b[i]]
        pltpu.make_async_remote_copy(half, half, f_send, f_left.at[i], to_right, MESH).start()
        share(block)
        block = gathered.at[right, :, c, column_b[i]]
        wait_bytes(block, x_right.at[i])
        half = gathered.at[right, pl.ds(2, 2), c, column_b[i]]
        pltpu.make_async_remote_copy(half, half, f_send, f_right.at[i], to_left, MESH).start()
        share(block)

    def take_across(i):
        wait_bytes(gathered.at[across, pl.ds(0, 2), c, column_b[i]], f_left.at[i])
        wait_bytes(gathered.at[across, pl.ds(2, 2), c, column_b[i]], f_right.at[i])
        share(gathered.at[across, :, c, column_b[i]])

    def forward(w, half):
        lhs = jnp.concatenate([slab[k, half * 512 : half * 512 + 512, :] for k in range(4)], axis=1)
        rhs = jnp.concatenate([arrived[w, :, m].reshape(2048, 128) for m in range(4)], axis=1)
        return jnp.dot(lhs, rhs, preferred_element_type=F32)

    def pass_copy(half):
        return pltpu.make_async_remote_copy(
            sent.at[0, half], passing.at[half], pass_send.at[half], pass_recv.at[half],
            to_left if half else to_right, MESH,
        )

    def partial_copy(w, half):
        return pltpu.make_async_remote_copy(
            sent.at[w, half], got.at[w - 1, half], p_send.at[w - 1, half], p_recv.at[w - 1, half],
            to_left if w == 2 else to_right, MESH,
        )

    stage(0)
    stage(1)
    barrier = pltpu.get_barrier_semaphore()
    peers = [device(x, (y + dy) % 4, (z + dz) % 4, c) for dy, dz in PLANE]
    stat_peers = [
        device(x, (y + dy) % 4, (z + dz) % 4, (c + dc) % 2)
        for dy in range(4) for dz in (0, 2) for dc in range(2) if dy or dz or dc
    ]
    cross_peers = [
        device(x, (y + dy) % 4, (z + dz) % 4, 1 - c) for dy in range(4) for dz in (0, 2)
    ]
    flipped = z + 1 - 2 * (z % 2)
    dp_peers = [device((x + dx) % 4, y, flipped, c) for dx in (1, 2, 3)]
    x_peers = [device((x + dx) % 4, y, z, c) for dx in (1, 2, 3)]
    everyone = peers + cross_peers + x_peers + dp_peers
    for peer in everyone:
        pl.semaphore_signal(barrier, 1, device_id=peer, device_id_type=MESH)

    turned = jnp.transpose(tokens[...])
    gathered[x, a, c, b] = turned
    wide = turned.astype(F32)
    t = lax.axis_index("tensor")
    stats[t] = jnp.broadcast_to(jnp.sum(wide * wide, axis=0, keepdims=True), (8, 128))
    pack(0)
    pl.semaphore_wait(barrier, len(everyone))
    mine = gathered.at[x, a, c, b]
    for i, d in enumerate((1, 3, 2)):
        pltpu.make_async_remote_copy(
            mine, mine, a_send, a_recv.at[i], at_ab((a + d) % 4, b), MESH
        ).start()
    send_block(a)
    their_copy(0).start()
    for peer in stat_peers:
        pltpu.make_async_remote_copy(
            stats.at[t], stats.at[t], stat_sem.at[0], stat_sem.at[1], peer, MESH
        ).start()
    pack(1)
    their_copy(1).start()
    for i, d in enumerate((3, 1, 2)):
        wait_bytes(gathered.at[x, (a + d) % 4, c, b], a_recv.at[i])
        send_block((a + d) % 4)
    share(gathered.at[x, :, c, b])
    send_wave(0)
    wait_bytes(stats.at[pl.ds(0, 15)], stat_sem.at[1])
    total = stats[0]
    for i in range(1, 16):
        total = total + stats[i]
    dp = lax.axis_index("dp")
    scales[dp] = lax.rsqrt(total * (1.0 / 8192.0) + epsilon)
    for peer in x_peers + dp_peers + [device(x, y, flipped, c)]:
        pltpu.make_async_remote_copy(
            scales.at[dp], scales.at[dp], scale_sem.at[0], scale_sem.at[1], peer, MESH
        ).start()
    send_column(1)
    send_column(2)
    send_column(3)
    send_wave(1)
    pack(2)
    their_copy(2).start()
    pass_on(0)
    send_wave(2)
    pack(3)
    their_copy(3).start()
    pass_on(1)
    take_across(0)
    send_wave(3)
    pass_on(2)
    take_across(1)
    pass_on(3)
    take_across(2)
    take_across(3)
    wait_bytes(gathered.at[:, :, 1 - c], d_recv)
    wait_bytes(scales.at[pl.ds(0, 7)], scale_sem.at[1])

    @pl.loop(0, 4)
    def _(from_x):
        for from_c in range(2):
            for from_z in range(4):
                dp = from_x * 2 + from_z % 2
                rows = pl.ds(pl.multiple_of(dp * 128, 128), 128)
                block = gathered[from_x, from_z, 1, x] if from_c else gathered[from_x, x, 0, from_z]
                block = (block.astype(F32) * scales[dp][:1]).astype(BF16)
                slab[(from_z // 2) * 2 + from_c, rows, :] = jnp.transpose(block)

    wait_bytes(arrived.at[0], wave_recv.at[0])
    for half in range(2):
        sent[0, half] = forward(0, half).astype(BF16)
        pass_copy(half).start()
    wait_bytes(arrived.at[1], wave_recv.at[1])
    sent[1, 1] = forward(1, 1).astype(BF16)
    partial_copy(1, 1).start()
    wait_bytes(arrived.at[2], wave_recv.at[2])
    sent[2, 0] = forward(2, 0).astype(BF16)
    partial_copy(2, 0).start()
    held[0] = forward(1, 0)
    held[1] = forward(2, 1)
    wait_bytes(gathered.at[0, 0, 0, pl.ds(0, 3)], a_send)
    wait_bytes(gathered.at[0, pl.ds(0, 3), 0], b_send)
    wait_bytes(gathered.at[0], x_send)
    wait_bytes(gathered.at[0, pl.ds(0, 2)], f_send)
    wait_bytes(gathered.at[pl.ds(0, 2)], d_send)
    normalise(0)
    normalise(1)
    pass_copy(0).wait_recv()
    sent[1, 0] = (held[0] + passing[0].astype(F32)).astype(BF16)
    partial_copy(1, 0).start()
    pass_copy(1).wait_recv()
    sent[2, 1] = (held[1] + passing[1].astype(F32)).astype(BF16)
    partial_copy(2, 1).start()
    normalise(2)
    normalise(3)
    wait_bytes(arrived.at[3], wave_recv.at[3])
    for half in range(2):
        sums[half] = forward(3, half)

    for w, half in ((1, 1), (2, 0), (1, 0), (2, 1)):
        partial_copy(w, half).wait_recv()

    for half in range(2):
        @pl.loop(0, 2)
        def _(part):
            rows = pl.ds(pl.multiple_of(part * 256, 256), 256)
            total = sums[half, rows, :] + (got[0, half, rows, :].astype(F32) + got[1, half, rows, :].astype(F32))
            to = pl.ds(pl.multiple_of(half * 512 + part * 256, 256), 256)
            gate_term, up_term = hidden_terms(total, adjoint[to, :])
            terms[to, :128] = gate_term
            terms[to, 128:] = up_term

    for half in range(2):
        pass_copy(half).wait_send()
        for w in (1, 2):
            partial_copy(w, half).wait_send()
    for w in range(4):
        wait_bytes(packed.at[w, pl.ds(0, 15)], wave_send.at[w])
    for w in (2, 3):
        their_copy(w).wait_send()
    wait_bytes(stats.at[pl.ds(0, 15)], stat_sem.at[0])
    wait_bytes(scales.at[pl.ds(0, 7)], scale_sem.at[0])


def product(gathered, terms, gate, up, gate_out, up_out, out_sem):
    def stores(t):
        rows = pl.ds(512 * t, 512)
        return (
            pltpu.make_async_copy(gate_out.at[t], gate.at[rows], out_sem.at[0, t]),
            pltpu.make_async_copy(up_out.at[t], up.at[rows], out_sem.at[1, t]),
        )

    for t in range(16):
        row, pair = t // 4, ((t // 2) % 2) * 2
        lhs = jnp.concatenate(
            [
                gathered[i, row, 0, pair + j] if t % 2 == 0 else gathered[i, pair + j, 1, row]
                for i in range(4)
                for j in range(2)
            ],
            axis=1,
        )
        result = jnp.dot(lhs, terms[...], preferred_element_type=F32)
        gate_out[t] = result[:, :128]
        up_out[t] = result[:, 128:]
        for store in stores(t):
            store.start()
    for t in range(16):
        for store in stores(t):
            store.wait()


def local(tokens, gate_weight, up_weight, gate_tangent, up_tangent, adjoint):
    dma = pltpu.SemaphoreType.DMA
    gathered, terms = pl.pallas_call(
        exchange,
        out_shape=(
            pltpu.VMEM((4, 4, 2, 4, 512, 128), BF16),
            pltpu.VMEM((1024, 256), BF16),
        ),
        in_specs=[pl.BlockSpec(memory_space=pltpu.VMEM)] * 2 + [pl.BlockSpec(memory_space=pl.ANY)] * 4,
        out_specs=(pl.BlockSpec(memory_space=pltpu.VMEM),) * 2,
        scratch_shapes=[
            pltpu.VMEM((2, 4, 64, 4096), BF16),
            pltpu.VMEM((2, 16, 4, 64, 128), BF16),
            pltpu.VMEM((4, 16, 4, 128, 128), BF16),
            pltpu.VMEM((4, 16, 4, 128, 128), BF16),
            pltpu.VMEM((16, 8, 128), F32),
            pltpu.VMEM((8, 8, 128), F32),
            pltpu.VMEM((4, 1024, 512), BF16),
            pltpu.VMEM((2, 512, 512), F32),
            pltpu.VMEM((2, 512, 512), F32),
            pltpu.VMEM((3, 2, 512, 512), BF16),
            pltpu.VMEM((2, 512, 512), BF16),
            pltpu.VMEM((2, 2, 512, 512), BF16),
            dma((2, 4)), dma((2,)), dma((4,)), dma((4,)), dma((4,)), dma((2,)), dma((2,)),
            dma, dma((3,)), dma, dma((3,)), dma, dma((4,)), dma((4,)), dma, dma((4,)), dma((4,)), dma, dma,
            dma((2,)), dma((2,)), dma((2, 2)), dma((2, 2)),
        ],
        compiler_params=pltpu.CompilerParams(
            collective_id=0, has_side_effects=True, vmem_limit_bytes=44 * 2**20
        ),
        name="exchange",
    )(tokens, adjoint, gate_weight, up_weight, gate_tangent, up_tangent)

    gathered = pltpu.with_memory_space_constraint(gathered, pltpu.VMEM)
    terms = pltpu.with_memory_space_constraint(terms, pltpu.VMEM)
    return pl.pallas_call(
        product,
        out_shape=(jax.ShapeDtypeStruct((8192, 128), F32),) * 2,
        in_specs=[pl.BlockSpec(memory_space=pltpu.VMEM)] * 2,
        out_specs=(pl.BlockSpec(memory_space=pl.ANY),) * 2,
        scratch_shapes=[
            pltpu.VMEM((16, 512, 128), F32),
            pltpu.VMEM((16, 512, 128), F32),
            dma((2, 16)),
        ],
        compiler_params=pltpu.CompilerParams(vmem_limit_bytes=24 * 2**20),
        name="product",
    )(gathered, terms)


def solution(mesh):
    in_specs = (
        P("dp", "tensor"),
        P(("dp", "tensor"), None),
        P(("dp", "tensor"), None),
        P(("dp", "tensor"), None),
        P(("dp", "tensor"), None),
        P(None, ("dp", "tensor")),
    )
    out_specs = (P(None, ("dp", "tensor")), P(None, ("dp", "tensor")))
    return jax.shard_map(local, mesh=mesh, in_specs=in_specs, out_specs=out_specs, check_vma=False)
```

```python
import jax
import jax.numpy as jnp
from jax import lax
from jax.experimental import pallas as pl
from jax.experimental.pallas import tpu as pltpu
from jax.sharding import PartitionSpec as P

epsilon = 1e-05
MESH = pl.DeviceIdType.MESH
BF16, F32 = jnp.bfloat16, jnp.float32
PLANE = (
    (1, 0), (0, 1), (3, 0), (0, 3), (2, 0), (0, 2), (1, 1), (3, 3),
    (1, 3), (3, 1), (1, 2), (2, 1), (3, 2), (2, 3), (2, 2),
)
WAVES = (
    ((0, 2), (1, 2), (2, 2), (3, 2)),
    ((0, 1), (1, 1), (0, 3), (1, 3)),
    ((2, 1), (3, 1), (2, 3), (3, 3)),
    ((0, 0), (1, 0), (2, 0), (3, 0)),
)


def place():
    dp, t = lax.axis_index("dp"), lax.axis_index("tensor")
    return dp // 2, t // 4, ((t // 2) % 2) * 2 + dp % 2, t % 2


def device(x, y, z, c):
    return (x * 2 + z % 2, (y * 2 + z // 2) * 2 + c)


def chip_in_plane(y, z):
    return (z % 2) * 8 + y * 2 + z // 2


def hidden_terms(forward, adjoint):
    gate_pre, up_pre = forward[:, :128], forward[:, 128:256]
    gate_dot, up_dot = forward[:, 256:384], forward[:, 384:]
    cotangent = adjoint.astype(F32)
    logistic = jax.nn.sigmoid(gate_pre)
    first = logistic * (1.0 + gate_pre * (1.0 - logistic))
    second = logistic * (1.0 - logistic) * (2.0 + gate_pre * (1.0 - 2.0 * logistic))
    gate_term = (cotangent * (up_dot * first + up_pre * second * gate_dot)).astype(BF16)
    up_term = (cotangent * first * gate_dot).astype(BF16)
    return gate_term, up_term


def exchange(
    tokens, adjoint, w0, w1, w2, w3, gathered, terms,
    held_tokens, held_adjoint, staged, theirs, packed, arrived, stats, scales, slab, sums, held, sent, passing, part, got,
    load_sem, stage_sem, their_send, their_recv, wave_send, wave_recv, stat_sem, scale_sem,
    a_send, a_recv, b_send, b_recv, x_send, x_left, x_right, f_send, f_left, f_right, d_send, d_recv,
    pass_send, pass_recv, p_send, p_recv,
):
    weights = (w0, w1, w2, w3)
    x, y, z, c = place()
    me = chip_in_plane(y, z)
    right, left, across = (x + 1) % 4, (x + 3) % 4, (x + 2) % 4
    partner = device(x, y, z, 1 - c)
    to_right, to_left = device(right, y, z, c), device(left, y, z, c)
    a, b = y * (1 - c) + z * c, z * (1 - c) + y * c

    def at_ab(to_a, to_b):
        return device(x, to_a * (1 - c) + to_b * c, to_b * (1 - c) + to_a * c, c)

    def stage_copies(w):
        copies = []
        for slot, (m, owner) in enumerate(WAVES[w]):
            start = pl.multiple_of(((x + owner) % 4) * 4096, 4096)
            copies.append(
                pltpu.make_async_copy(
                    weights[m].at[:, pl.ds(start, 4096)],
                    staged.at[w % 2, slot],
                    stage_sem.at[w % 2, slot],
                )
            )
        return copies

    def stage(w):
        for copy in stage_copies(w):
            copy.start()

    def their_copy(w):
        return pltpu.make_async_remote_copy(
            theirs.at[w % 2],
            packed.at[w, :, :, pl.ds(pl.multiple_of(c * 64, 64), 64), :],
            their_send.at[w % 2],
            their_recv.at[w],
            partner,
            MESH,
        )

    def pack(w):
        for copy in stage_copies(w):
            copy.wait()
        if w >= 2:
            their_copy(w - 2).wait_send()

        @pl.loop(0, 16)
        def _(q):
            for m in range(4):
                both = staged[w % 2, m, :, pl.ds(pl.multiple_of(q * 256, 256), 256)]
                low, high = both[:, :128], both[:, 128:]
                packed[w, q, m, pl.ds(pl.multiple_of(c * 64, 64), 64), :] = jnp.where(c == 0, low, high)
                theirs[w % 2, q, m] = jnp.where(c == 0, high, low)

        if w + 2 < 4:
            stage(w + 2)

    def send_wave(w):
        their_copy(w).wait_recv()
        for dy, dz in PLANE:
            to_y = (y + dy * (1 - c) + (4 - dz) * c) % 4
            to_z = (z + dz * (1 - c) + (4 - dy) * c) % 4
            pltpu.make_async_remote_copy(
                packed.at[w, chip_in_plane(to_y, to_z)],
                arrived.at[w, me],
                wave_send.at[w],
                wave_recv.at[w],
                device(x, to_y, to_z, c),
                MESH,
            ).start()
        pltpu.make_async_copy(packed.at[w, me], arrived.at[w, me], wave_recv.at[w]).start()

    def wait_bytes(ref, sem):
        pltpu.make_async_copy(ref, ref, sem).wait()

    def share(block, r):
        pltpu.make_async_remote_copy(block, block, d_send, d_recv.at[r], partner, MESH).start()

    column_b = [b, (b + 3) % 4, (b + 1) % 4, (b + 2) % 4]

    def send_x(i, block):
        pltpu.make_async_remote_copy(block, block, x_send, x_left.at[i], to_right, MESH).start()
        pltpu.make_async_remote_copy(block, block, x_send, x_right.at[i], to_left, MESH).start()

    block_a = [a, (a + 3) % 4, (a + 1) % 4, (a + 2) % 4]

    def send_block(k):
        block = gathered.at[x, block_a[k], c, b]
        if k > 0:
            wait_bytes(block, a_recv.at[k - 1])
        for i, d in enumerate((1, 3, 2)):
            pltpu.make_async_remote_copy(
                block, block, b_send, b_recv.at[i, k], at_ab(a, (b + d) % 4), MESH
            ).start()
        send_x(0, block)

    def relay_block(i, k):
        block = gathered.at[x, block_a[k], c, column_b[i]]
        wait_bytes(block, b_recv.at[i - 1, k])
        send_x(i, block)

    def normalise(from_x):
        @pl.loop(0, 16)
        def _(i):
            at_a, at_b = i // 4, i % 4
            for from_c in range(2):
                from_z = at_a if from_c else at_b
                scale = scales[from_x * 2 + from_z % 2][:1]
                block = gathered[from_x, at_a, from_c, at_b].astype(F32)
                gathered[from_x, at_a, from_c, at_b] = (block * scale).astype(BF16)

    def pass_on(i):
        block = gathered.at[left, :, c, column_b[i]]
        wait_bytes(block, x_left.at[i])
        half = gathered.at[left, pl.ds(0, 2), c, column_b[i]]
        pltpu.make_async_remote_copy(half, half, f_send, f_left.at[i], to_right, MESH).start()
        share(block, 1)
        block = gathered.at[right, :, c, column_b[i]]
        wait_bytes(block, x_right.at[i])
        half = gathered.at[right, pl.ds(2, 2), c, column_b[i]]
        pltpu.make_async_remote_copy(half, half, f_send, f_right.at[i], to_left, MESH).start()
        share(block, 2)

    def take_across(i):
        wait_bytes(gathered.at[across, pl.ds(0, 2), c, column_b[i]], f_left.at[i])
        wait_bytes(gathered.at[across, pl.ds(2, 2), c, column_b[i]], f_right.at[i])
        share(gathered.at[across, :, c, column_b[i]], 3)

    def forward(w, rows):
        lhs = jnp.concatenate([slab[k, rows, :] for k in range(4)], axis=1)
        rhs = jnp.concatenate([arrived[w, :, m].reshape(2048, 128) for m in range(4)], axis=1)
        return jnp.dot(lhs, rhs, preferred_element_type=F32)

    def quarter(q):
        return pl.ds(pl.multiple_of(q * 256, 256), 256)

    def x_neighbour(way):
        return device((x + 1 + 2 * way) % 4, y, z, c)

    def make_slab(q, r):
        wait_bytes(gathered.at[q, :, 1 - c], d_recv.at[r])
        for from_z in range(4):
            for from_c in range(2):
                rows = pl.ds(pl.multiple_of(q * 256 + from_z % 2 * 128, 128), 128)
                scale = scales[q * 2 + from_z % 2][:1]
                block = gathered[q, from_z, 1, x] if from_c else gathered[q, x, 0, from_z]
                block = (block.astype(F32) * scale).astype(BF16)
                slab[(from_z // 2) * 2 + from_c, rows, :] = jnp.transpose(block)

    def pass_copy(q):
        return pltpu.make_async_remote_copy(
            sent.at[q], passing.at[q], pass_send.at[q], pass_recv.at[q], x_neighbour(q // 2), MESH
        )

    def forward_across(q):
        sent[q] = forward(0, quarter(q)).astype(BF16)
        pass_copy(q).start()

    def part_copy(w, q, late, way):
        pltpu.make_async_remote_copy(
            part.at[w - 1, late, q], got.at[w - 1, way, q], p_send, p_recv.at[q], x_neighbour(way), MESH
        ).start()

    def forward_beside(w, q):
        total = forward(w, quarter(q))
        to_r, to_l = total[:, :256], total[:, 256:]
        way = q // 2
        part[w - 1, 0, q] = jnp.where(way == 0, to_l, to_r).astype(BF16)
        part_copy(w, q, 0, 1 - way)
        held[w - 1, q] = jnp.where(way == 0, to_r, to_l)

    def add_passing(w, q):
        add = passing[q, :, (w - 1) * 256 : w * 256].astype(F32)
        part[w - 1, 1, q] = (held[w - 1, q] + add).astype(BF16)
        part_copy(w, q, 1, q // 2)

    barrier = pltpu.get_barrier_semaphore()
    peers = [device(x, (y + dy) % 4, (z + dz) % 4, c) for dy, dz in PLANE]
    stat_peers = [
        device(x, (y + dy) % 4, (z + dz) % 4, (c + dc) % 2)
        for dy in range(4) for dz in (0, 2) for dc in range(2) if dy or dz or dc
    ]
    cross_peers = [
        device(x, (y + dy) % 4, (z + dz) % 4, 1 - c) for dy in range(4) for dz in (0, 2)
    ]
    flipped = z + 1 - 2 * (z % 2)
    dp_peers = [device((x + dx) % 4, y, flipped, c) for dx in (1, 2, 3)]
    x_peers = [device((x + dx) % 4, y, z, c) for dx in (1, 2, 3)]
    everyone = peers + cross_peers + x_peers + dp_peers
    for peer in everyone:
        pl.semaphore_signal(barrier, 1, device_id=peer, device_id_type=MESH)

    load_tokens = pltpu.make_async_copy(tokens, held_tokens, load_sem.at[0])
    load_tokens.start()
    load_adjoint = pltpu.make_async_copy(adjoint, held_adjoint, load_sem.at[1])
    load_adjoint.start()
    stage(0)
    stage(1)
    load_tokens.wait()
    turned = jnp.transpose(held_tokens[...])
    mine = gathered.at[x, a, c, b]
    mine[...] = turned
    pl.semaphore_wait(barrier, len(everyone))
    for i, d in enumerate((1, 3, 2)):
        pltpu.make_async_remote_copy(
            mine, mine, a_send, a_recv.at[i], at_ab((a + d) % 4, b), MESH
        ).start()
    send_block(0)
    wide = turned.astype(F32)
    t = lax.axis_index("tensor")
    stats[t] = jnp.broadcast_to(jnp.sum(wide * wide, axis=0, keepdims=True), (8, 128))
    for peer in stat_peers:
        pltpu.make_async_remote_copy(
            stats.at[t], stats.at[t], stat_sem.at[0], stat_sem.at[1], peer, MESH
        ).start()
    pack(0)
    their_copy(0).start()
    send_block(1)
    send_block(2)
    relay_block(1, 0)
    relay_block(2, 0)
    send_block(3)
    relay_block(3, 0)
    share(gathered.at[x, :, c, b], 0)
    send_wave(0)
    pack(1)
    their_copy(1).start()
    wait_bytes(stats.at[pl.ds(0, 15)], stat_sem.at[1])
    total = stats[0]
    for i in range(1, 16):
        total = total + stats[i]
    dp = lax.axis_index("dp")
    scales[dp] = lax.rsqrt(total * (1.0 / 8192.0) + epsilon)
    for peer in x_peers + dp_peers + [device(x, y, flipped, c)]:
        pltpu.make_async_remote_copy(
            scales.at[dp], scales.at[dp], scale_sem.at[0], scale_sem.at[1], peer, MESH
        ).start()
    for k in (1, 2, 3):
        for i in (1, 2, 3):
            relay_block(i, k)
    for i in (1, 2, 3):
        share(gathered.at[x, :, c, column_b[i]], 0)
    send_wave(1)
    pack(2)
    their_copy(2).start()
    pass_on(0)
    send_wave(2)
    pack(3)
    their_copy(3).start()
    wait_bytes(scales.at[pl.ds(0, 7)], scale_sem.at[1])
    make_slab(x, 0)
    pass_on(1)
    take_across(0)
    send_wave(3)
    wait_bytes(arrived.at[0], wave_recv.at[0])
    forward_across(x)
    pass_on(2)
    take_across(1)
    pass_on(3)
    make_slab(left, 1)
    forward_across(left)
    make_slab(right, 2)
    forward_across(right)
    take_across(2)
    take_across(3)
    wait_bytes(arrived.at[1], wave_recv.at[1])
    forward_beside(1, x)
    forward_beside(1, left)
    forward_beside(1, right)
    make_slab(across, 3)
    forward_across(across)
    forward_beside(1, across)
    wait_bytes(gathered.at[0, 0, 0, pl.ds(0, 3)], a_send)
    wait_bytes(gathered.at[0, pl.ds(0, 3), 0], b_send)
    wait_bytes(gathered.at[0], x_send)
    wait_bytes(gathered.at[0, pl.ds(0, 2)], f_send)
    wait_bytes(gathered.at[pl.ds(0, 2)], d_send)

    @pl.loop(0, 4)
    def _(q):
        pass_copy(q).wait_recv()
        add_passing(1, q)
        normalise(q)

    wait_bytes(arrived.at[2], wave_recv.at[2])

    @pl.loop(0, 4)
    def _(q):
        forward_beside(2, q)
        add_passing(2, q)

    wait_bytes(arrived.at[3], wave_recv.at[3])
    for half in range(2):
        rows = pl.ds(half * 512, 512)
        sums[rows, :] = forward(3, rows)

    load_adjoint.wait()

    @pl.loop(0, 4)
    def _(q):
        wait_bytes(got.at[0, :, pl.ds(0, 2)], p_recv.at[q])
        total = sums[quarter(q), :]
        for way in range(2):
            total = total + jnp.concatenate([got[0, way, q], got[1, way, q]], axis=1).astype(F32)
        gate_term, up_term = hidden_terms(total, held_adjoint[quarter(q), :])
        terms[quarter(q), :128] = gate_term
        terms[quarter(q), 128:] = up_term

    for q in range(4):
        pass_copy(q).wait_send()
    wait_bytes(part, p_send)
    for w in range(4):
        wait_bytes(packed.at[w, pl.ds(0, 15)], wave_send.at[w])
    for w in (2, 3):
        their_copy(w).wait_send()
    wait_bytes(stats.at[pl.ds(0, 15)], stat_sem.at[0])
    wait_bytes(scales.at[pl.ds(0, 7)], scale_sem.at[0])


def product(gathered, terms, gate, up, gate_out, up_out, out_sem):
    def stores(t):
        rows = pl.ds(512 * t, 512)
        return (
            pltpu.make_async_copy(gate_out.at[t], gate.at[rows], out_sem.at[0, t]),
            pltpu.make_async_copy(up_out.at[t], up.at[rows], out_sem.at[1, t]),
        )

    for t in range(16):
        row, pair = t // 4, ((t // 2) % 2) * 2
        lhs = jnp.concatenate(
            [
                gathered[i, row, 0, pair + j] if t % 2 == 0 else gathered[i, pair + j, 1, row]
                for i in range(4)
                for j in range(2)
            ],
            axis=1,
        )
        result = jnp.dot(lhs, terms[...], preferred_element_type=F32)
        gate_out[t] = result[:, :128]
        up_out[t] = result[:, 128:]
        for store in stores(t):
            store.start()
    for t in range(16):
        for store in stores(t):
            store.wait()


def local(tokens, gate_weight, up_weight, gate_tangent, up_tangent, adjoint):
    dma = pltpu.SemaphoreType.DMA
    gathered, terms = pl.pallas_call(
        exchange,
        out_shape=(
            pltpu.VMEM((4, 4, 2, 4, 512, 128), BF16),
            pltpu.VMEM((1024, 256), BF16),
        ),
        in_specs=[pl.BlockSpec(memory_space=pl.ANY)] * 6,
        out_specs=(pl.BlockSpec(memory_space=pltpu.VMEM),) * 2,
        scratch_shapes=[
            pltpu.VMEM((128, 512), BF16),
            pltpu.VMEM((1024, 128), BF16),
            pltpu.VMEM((2, 4, 64, 4096), BF16),
            pltpu.VMEM((2, 16, 4, 64, 128), BF16),
            pltpu.VMEM((4, 16, 4, 128, 128), BF16),
            pltpu.VMEM((4, 16, 4, 128, 128), BF16),
            pltpu.VMEM((16, 8, 128), F32),
            pltpu.VMEM((8, 8, 128), F32),
            pltpu.VMEM((4, 1024, 512), BF16),
            pltpu.VMEM((1024, 512), F32),
            pltpu.VMEM((2, 4, 256, 256), F32),
            pltpu.VMEM((4, 256, 512), BF16),
            pltpu.VMEM((4, 256, 512), BF16),
            pltpu.VMEM((2, 2, 4, 256, 256), BF16),
            pltpu.VMEM((2, 2, 4, 256, 256), BF16),
            dma((2,)), dma((2, 4)), dma((2,)), dma((4,)), dma((4,)), dma((4,)), dma((2,)), dma((2,)),
            dma, dma((3,)), dma, dma((3, 4)), dma, dma((4,)), dma((4,)), dma, dma((4,)), dma((4,)), dma, dma((4,)),
            dma((4,)), dma((4,)), dma, dma((4,)),
        ],
        compiler_params=pltpu.CompilerParams(
            collective_id=0, has_side_effects=True, vmem_limit_bytes=44 * 2**20
        ),
        name="exchange",
    )(tokens, adjoint, gate_weight, up_weight, gate_tangent, up_tangent)

    gathered = pltpu.with_memory_space_constraint(gathered, pltpu.VMEM)
    terms = pltpu.with_memory_space_constraint(terms, pltpu.VMEM)
    return pl.pallas_call(
        product,
        out_shape=(jax.ShapeDtypeStruct((8192, 128), F32),) * 2,
        in_specs=[pl.BlockSpec(memory_space=pltpu.VMEM)] * 2,
        out_specs=(pl.BlockSpec(memory_space=pl.ANY),) * 2,
        scratch_shapes=[
            pltpu.VMEM((16, 512, 128), F32),
            pltpu.VMEM((16, 512, 128), F32),
            dma((2, 16)),
        ],
        compiler_params=pltpu.CompilerParams(vmem_limit_bytes=24 * 2**20),
        name="product",
    )(gathered, terms)


def solution(mesh):
    in_specs = (
        P("dp", "tensor"),
        P(("dp", "tensor"), None),
        P(("dp", "tensor"), None),
        P(("dp", "tensor"), None),
        P(("dp", "tensor"), None),
        P(None, ("dp", "tensor")),
    )
    out_specs = (P(None, ("dp", "tensor")), P(None, ("dp", "tensor")))
    return jax.shard_map(local, mesh=mesh, in_specs=in_specs, out_specs=out_specs, check_vma=False)
```

```python
import jax
import jax.numpy as jnp
from jax import lax
from jax.experimental import pallas as pl
from jax.experimental.pallas import tpu as pltpu
from jax.sharding import PartitionSpec as P

epsilon = 1e-05
MESH = pl.DeviceIdType.MESH
BF16, F32 = jnp.bfloat16, jnp.float32
PLANE = (
    (1, 0), (0, 1), (3, 0), (0, 3), (2, 0), (0, 2), (1, 1), (3, 3),
    (1, 3), (3, 1), (1, 2), (2, 1), (3, 2), (2, 3), (2, 2),
)
WAVES = (
    ((0, 2), (1, 2), (2, 2), (3, 2)),
    ((0, 1), (1, 1), (0, 3), (1, 3)),
    ((2, 1), (3, 1), (2, 3), (3, 3)),
    ((0, 0), (1, 0), (2, 0), (3, 0)),
)


def place():
    dp, t = lax.axis_index("dp"), lax.axis_index("tensor")
    return dp // 2, t // 4, ((t // 2) % 2) * 2 + dp % 2, t % 2


def device(x, y, z, c):
    return (x * 2 + z % 2, (y * 2 + z // 2) * 2 + c)


def chip_in_plane(y, z):
    return (z % 2) * 8 + y * 2 + z // 2


def hidden_terms(forward, adjoint):
    gate_pre, up_pre = forward[:, :128], forward[:, 128:256]
    gate_dot, up_dot = forward[:, 256:384], forward[:, 384:]
    cotangent = adjoint.astype(F32)
    logistic = jax.nn.sigmoid(gate_pre)
    first = logistic * (1.0 + gate_pre * (1.0 - logistic))
    second = logistic * (1.0 - logistic) * (2.0 + gate_pre * (1.0 - 2.0 * logistic))
    gate_term = (cotangent * (up_dot * first + up_pre * second * gate_dot)).astype(BF16)
    up_term = (cotangent * first * gate_dot).astype(BF16)
    return gate_term, up_term


def exchange(
    tokens, adjoint, w0, w1, w2, w3, gathered, terms,
    held_tokens, held_adjoint, staged, theirs, packed, arrived, stats, scales, slab, sums, held, sent, passing, part, got,
    load_sem, stage_sem, their_send, their_recv, wave_send, wave_recv, stat_sem, scale_sem,
    a_send, a_recv, b_send, b_recv, x_send, x_left, x_right, f_send, f_left, f_right, d_send, d_recv,
    pass_send, pass_recv, p_send, p_recv,
):
    weights = (w0, w1, w2, w3)
    x, y, z, c = place()
    me = chip_in_plane(y, z)
    right, left, across = (x + 1) % 4, (x + 3) % 4, (x + 2) % 4
    partner = device(x, y, z, 1 - c)
    to_right, to_left = device(right, y, z, c), device(left, y, z, c)
    a, b = y * (1 - c) + z * c, z * (1 - c) + y * c

    def at_ab(to_a, to_b):
        return device(x, to_a * (1 - c) + to_b * c, to_b * (1 - c) + to_a * c, c)

    def stage_copies(w):
        copies = []
        for slot, (m, owner) in enumerate(WAVES[w]):
            start = pl.multiple_of(((x + owner) % 4) * 4096, 4096)
            copies.append(
                pltpu.make_async_copy(
                    weights[m].at[:, pl.ds(start, 4096)],
                    staged.at[w % 2, slot],
                    stage_sem.at[w % 2, slot],
                )
            )
        return copies

    def stage(w):
        for copy in stage_copies(w):
            copy.start()

    def their_copy(w):
        return pltpu.make_async_remote_copy(
            theirs.at[w % 2],
            packed.at[w, :, :, pl.ds(pl.multiple_of(c * 64, 64), 64), :],
            their_send.at[w % 2],
            their_recv.at[w],
            partner,
            MESH,
        )

    def pack(w):
        for copy in stage_copies(w):
            copy.wait()
        if w >= 2:
            their_copy(w - 2).wait_send()

        @pl.loop(0, 16)
        def _(q):
            for m in range(4):
                both = staged[w % 2, m, :, pl.ds(pl.multiple_of(q * 256, 256), 256)]
                low, high = both[:, :128], both[:, 128:]
                packed[w, q, m, pl.ds(pl.multiple_of(c * 64, 64), 64), :] = jnp.where(c == 0, low, high)
                theirs[w % 2, q, m] = jnp.where(c == 0, high, low)

        if w + 2 < 4:
            stage(w + 2)

    def send_wave(w, slots=(0, 4), sem=None):
        slots, sem = pl.ds(slots[0], slots[1]), w if sem is None else sem
        if sem == w:
            their_copy(w).wait_recv()
        for dy, dz in PLANE:
            to_y = (y + dy * (1 - c) + (4 - dz) * c) % 4
            to_z = (z + dz * (1 - c) + (4 - dy) * c) % 4
            pltpu.make_async_remote_copy(
                packed.at[w, chip_in_plane(to_y, to_z), slots],
                arrived.at[w, me, slots],
                wave_send.at[w],
                wave_recv.at[sem],
                device(x, to_y, to_z, c),
                MESH,
            ).start()
        pltpu.make_async_copy(
            packed.at[w, me, slots], arrived.at[w, me, slots], wave_recv.at[sem]
        ).start()

    def wait_bytes(ref, sem):
        pltpu.make_async_copy(ref, ref, sem).wait()

    def share(block, r):
        pltpu.make_async_remote_copy(block, block, d_send, d_recv.at[r], partner, MESH).start()

    column_b = [b, (b + 3) % 4, (b + 1) % 4, (b + 2) % 4]

    def send_x(i, block):
        pltpu.make_async_remote_copy(block, block, x_send, x_left.at[i], to_right, MESH).start()
        pltpu.make_async_remote_copy(block, block, x_send, x_right.at[i], to_left, MESH).start()

    block_a = [a, (a + 3) % 4, (a + 1) % 4, (a + 2) % 4]

    def send_block(k):
        block = gathered.at[x, block_a[k], c, b]
        if k > 0:
            wait_bytes(block, a_recv.at[k - 1])
        for i, d in enumerate((1, 3, 2)):
            pltpu.make_async_remote_copy(
                block, block, b_send, b_recv.at[i, k], at_ab(a, (b + d) % 4), MESH
            ).start()
        send_x(0, block)

    def relay_block(i, k):
        block = gathered.at[x, block_a[k], c, column_b[i]]
        wait_bytes(block, b_recv.at[i - 1, k])
        send_x(i, block)

    def normalise(from_x):
        @pl.loop(0, 16)
        def _(i):
            at_a, at_b = i // 4, i % 4
            for from_c in range(2):
                from_z = at_a if from_c else at_b
                scale = scales[from_x * 2 + from_z % 2][:1]
                block = gathered[from_x, at_a, from_c, at_b].astype(F32)
                gathered[from_x, at_a, from_c, at_b] = (block * scale).astype(BF16)

    def pass_on(i):
        block = gathered.at[left, :, c, column_b[i]]
        wait_bytes(block, x_left.at[i])
        half = gathered.at[left, pl.ds(0, 2), c, column_b[i]]
        pltpu.make_async_remote_copy(half, half, f_send, f_left.at[i], to_right, MESH).start()
        share(block, 1)
        block = gathered.at[right, :, c, column_b[i]]
        wait_bytes(block, x_right.at[i])
        half = gathered.at[right, pl.ds(2, 2), c, column_b[i]]
        pltpu.make_async_remote_copy(half, half, f_send, f_right.at[i], to_left, MESH).start()
        share(block, 2)

    def take_across(i):
        wait_bytes(gathered.at[across, pl.ds(0, 2), c, column_b[i]], f_left.at[i])
        wait_bytes(gathered.at[across, pl.ds(2, 2), c, column_b[i]], f_right.at[i])
        share(gathered.at[across, :, c, column_b[i]], 3)

    def forward(w, rows, slots=range(4)):
        lhs = jnp.concatenate([slab[k, rows, :] for k in range(4)], axis=1)
        rhs = jnp.concatenate([arrived[w, :, m].reshape(2048, 128) for m in slots], axis=1)
        return jnp.dot(lhs, rhs, preferred_element_type=F32)

    def quarter(q):
        return pl.ds(pl.multiple_of(q * 256, 256), 256)

    def x_neighbour(way):
        return device((x + 1 + 2 * way) % 4, y, z, c)

    def make_slab(q, r):
        wait_bytes(gathered.at[q, :, 1 - c], d_recv.at[r])
        for from_z in range(4):
            for from_c in range(2):
                rows = pl.ds(pl.multiple_of(q * 256 + from_z % 2 * 128, 128), 128)
                scale = scales[q * 2 + from_z % 2][:1]
                block = gathered[q, from_z, 1, x] if from_c else gathered[q, x, 0, from_z]
                block = (block.astype(F32) * scale).astype(BF16)
                slab[(from_z // 2) * 2 + from_c, rows, :] = jnp.transpose(block)

    def pass_copy(q):
        return pltpu.make_async_remote_copy(
            sent.at[q], passing.at[q], pass_send.at[q], pass_recv.at[q], x_neighbour(q // 2), MESH
        )

    def forward_across(q):
        sent[q] = forward(0, quarter(q)).astype(BF16)
        pass_copy(q).start()

    def part_copy(w, q, late, way):
        pltpu.make_async_remote_copy(
            part.at[w - 1, late, q], got.at[w - 1, way, q], p_send, p_recv.at[q], x_neighbour(way), MESH
        ).start()

    def forward_beside(w, q):
        total = forward(w, quarter(q))
        to_r, to_l = total[:, :256], total[:, 256:]
        way = q // 2
        part[w - 1, 0, q] = jnp.where(way == 0, to_l, to_r).astype(BF16)
        part_copy(w, q, 0, 1 - way)
        held[w - 1, q] = jnp.where(way == 0, to_r, to_l)

    def add_passing(w, q):
        add = passing[q, :, (w - 1) * 256 : w * 256].astype(F32)
        part[w - 1, 1, q] = (held[w - 1, q] + add).astype(BF16)
        part_copy(w, q, 1, q // 2)

    barrier = pltpu.get_barrier_semaphore()
    peers = [device(x, (y + dy) % 4, (z + dz) % 4, c) for dy, dz in PLANE]
    stat_peers = [
        device(x, (y + dy) % 4, (z + dz) % 4, (c + dc) % 2)
        for dy in range(4) for dz in (0, 2) for dc in range(2) if dy or dz or dc
    ]
    cross_peers = [
        device(x, (y + dy) % 4, (z + dz) % 4, 1 - c) for dy in range(4) for dz in (0, 2)
    ]
    flipped = z + 1 - 2 * (z % 2)
    dp_peers = [device((x + dx) % 4, y, flipped, c) for dx in (1, 2, 3)]
    x_peers = [device((x + dx) % 4, y, z, c) for dx in (1, 2, 3)]
    everyone = peers + cross_peers + x_peers + dp_peers
    for peer in everyone:
        pl.semaphore_signal(barrier, 1, device_id=peer, device_id_type=MESH)

    load_tokens = pltpu.make_async_copy(tokens, held_tokens, load_sem.at[0])
    load_tokens.start()
    load_adjoint = pltpu.make_async_copy(adjoint, held_adjoint, load_sem.at[1])
    load_adjoint.start()
    stage(0)
    stage(1)
    load_tokens.wait()
    turned = jnp.transpose(held_tokens[...])
    mine = gathered.at[x, a, c, b]
    mine[...] = turned
    pl.semaphore_wait(barrier, len(everyone))
    for i, d in enumerate((1, 3, 2)):
        pltpu.make_async_remote_copy(
            mine, mine, a_send, a_recv.at[i], at_ab((a + d) % 4, b), MESH
        ).start()
    send_block(0)
    wide = turned.astype(F32)
    t = lax.axis_index("tensor")
    stats[t] = jnp.broadcast_to(jnp.sum(wide * wide, axis=0, keepdims=True), (8, 128))
    for peer in stat_peers:
        pltpu.make_async_remote_copy(
            stats.at[t], stats.at[t], stat_sem.at[0], stat_sem.at[1], peer, MESH
        ).start()
    pack(0)
    their_copy(0).start()
    send_block(1)
    send_block(2)
    relay_block(1, 0)
    relay_block(2, 0)
    send_block(3)
    relay_block(3, 0)
    share(gathered.at[x, :, c, b], 0)
    send_wave(0)
    pack(1)
    their_copy(1).start()
    wait_bytes(stats.at[pl.ds(0, 15)], stat_sem.at[1])
    total = stats[0]
    for i in range(1, 16):
        total = total + stats[i]
    dp = lax.axis_index("dp")
    scales[dp] = lax.rsqrt(total * (1.0 / 8192.0) + epsilon)
    for peer in x_peers + dp_peers + [device(x, y, flipped, c)]:
        pltpu.make_async_remote_copy(
            scales.at[dp], scales.at[dp], scale_sem.at[0], scale_sem.at[1], peer, MESH
        ).start()
    for k in (1, 2, 3):
        for i in (1, 2, 3):
            relay_block(i, k)
    for i in (1, 2, 3):
        share(gathered.at[x, :, c, column_b[i]], 0)
    send_wave(1)
    pack(2)
    their_copy(2).start()
    pass_on(0)
    send_wave(2)
    pack(3)
    their_copy(3).start()
    wait_bytes(scales.at[pl.ds(0, 7)], scale_sem.at[1])
    make_slab(x, 0)
    pass_on(1)
    take_across(0)
    send_wave(3, (0, 2))
    send_wave(3, (2, 2), 4)
    wait_bytes(arrived.at[0], wave_recv.at[0])
    forward_across(x)
    pass_on(2)
    take_across(1)
    pass_on(3)
    make_slab(left, 1)
    forward_across(left)
    make_slab(right, 2)
    forward_across(right)
    take_across(2)
    take_across(3)
    wait_bytes(arrived.at[1], wave_recv.at[1])
    forward_beside(1, x)
    forward_beside(1, left)
    forward_beside(1, right)
    make_slab(across, 3)
    forward_across(across)
    forward_beside(1, across)
    @pl.loop(0, 4)
    def _(q):
        pass_copy(q).wait_recv()
        add_passing(1, q)

    wait_bytes(arrived.at[2], wave_recv.at[2])

    @pl.loop(0, 4)
    def _(q):
        forward_beside(2, q)
        add_passing(2, q)

    wait_bytes(gathered.at[0, 0, 0, pl.ds(0, 3)], a_send)
    wait_bytes(gathered.at[0, pl.ds(0, 3), 0], b_send)
    wait_bytes(gathered.at[0], x_send)
    wait_bytes(gathered.at[0, pl.ds(0, 2)], f_send)
    wait_bytes(gathered.at[pl.ds(0, 2)], d_send)

    @pl.loop(0, 4)
    def _(q):
        normalise(q)

    for pair in range(2):
        wait_bytes(arrived.at[3, :, pl.ds(pair * 2, 2)], wave_recv.at[3 + pair])
        for half in range(2):
            rows = pl.ds(half * 512, 512)
            sums[rows, pair * 256 : pair * 256 + 256] = forward(3, rows, (pair * 2, pair * 2 + 1))

    load_adjoint.wait()

    @pl.loop(0, 4)
    def _(q):
        wait_bytes(got.at[0, :, pl.ds(0, 2)], p_recv.at[q])
        total = sums[quarter(q), :]
        for way in range(2):
            total = total + jnp.concatenate([got[0, way, q], got[1, way, q]], axis=1).astype(F32)
        gate_term, up_term = hidden_terms(total, held_adjoint[quarter(q), :])
        terms[quarter(q), :128] = gate_term
        terms[quarter(q), 128:] = up_term

    for q in range(4):
        pass_copy(q).wait_send()
    wait_bytes(part, p_send)
    for w in range(4):
        wait_bytes(packed.at[w, pl.ds(0, 15)], wave_send.at[w])
    for w in (2, 3):
        their_copy(w).wait_send()
    wait_bytes(stats.at[pl.ds(0, 15)], stat_sem.at[0])
    wait_bytes(scales.at[pl.ds(0, 7)], scale_sem.at[0])


def product(gathered, terms, gate, up, gate_out, up_out, out_sem):
    def stores(t):
        rows = pl.ds(512 * t, 512)
        return (
            pltpu.make_async_copy(gate_out.at[t], gate.at[rows], out_sem.at[0, t]),
            pltpu.make_async_copy(up_out.at[t], up.at[rows], out_sem.at[1, t]),
        )

    for t in range(16):
        row, pair = t // 4, ((t // 2) % 2) * 2
        lhs = jnp.concatenate(
            [
                gathered[i, row, 0, pair + j] if t % 2 == 0 else gathered[i, pair + j, 1, row]
                for i in range(4)
                for j in range(2)
            ],
            axis=1,
        )
        result = jnp.dot(lhs, terms[...], preferred_element_type=F32)
        gate_out[t] = result[:, :128]
        up_out[t] = result[:, 128:]
        for store in stores(t):
            store.start()
    for t in range(16):
        for store in stores(t):
            store.wait()


def local(tokens, gate_weight, up_weight, gate_tangent, up_tangent, adjoint):
    dma = pltpu.SemaphoreType.DMA
    gathered, terms = pl.pallas_call(
        exchange,
        out_shape=(
            pltpu.VMEM((4, 4, 2, 4, 512, 128), BF16),
            pltpu.VMEM((1024, 256), BF16),
        ),
        in_specs=[pl.BlockSpec(memory_space=pl.ANY)] * 6,
        out_specs=(pl.BlockSpec(memory_space=pltpu.VMEM),) * 2,
        scratch_shapes=[
            pltpu.VMEM((128, 512), BF16),
            pltpu.VMEM((1024, 128), BF16),
            pltpu.VMEM((2, 4, 64, 4096), BF16),
            pltpu.VMEM((2, 16, 4, 64, 128), BF16),
            pltpu.VMEM((4, 16, 4, 128, 128), BF16),
            pltpu.VMEM((4, 16, 4, 128, 128), BF16),
            pltpu.VMEM((16, 8, 128), F32),
            pltpu.VMEM((8, 8, 128), F32),
            pltpu.VMEM((4, 1024, 512), BF16),
            pltpu.VMEM((1024, 512), F32),
            pltpu.VMEM((2, 4, 256, 256), F32),
            pltpu.VMEM((4, 256, 512), BF16),
            pltpu.VMEM((4, 256, 512), BF16),
            pltpu.VMEM((2, 2, 4, 256, 256), BF16),
            pltpu.VMEM((2, 2, 4, 256, 256), BF16),
            dma((2,)), dma((2, 4)), dma((2,)), dma((4,)), dma((4,)), dma((5,)), dma((2,)), dma((2,)),
            dma, dma((3,)), dma, dma((3, 4)), dma, dma((4,)), dma((4,)), dma, dma((4,)), dma((4,)), dma, dma((4,)),
            dma((4,)), dma((4,)), dma, dma((4,)),
        ],
        compiler_params=pltpu.CompilerParams(
            collective_id=0, has_side_effects=True, vmem_limit_bytes=44 * 2**20
        ),
        name="exchange",
    )(tokens, adjoint, gate_weight, up_weight, gate_tangent, up_tangent)

    gathered = pltpu.with_memory_space_constraint(gathered, pltpu.VMEM)
    terms = pltpu.with_memory_space_constraint(terms, pltpu.VMEM)
    return pl.pallas_call(
        product,
        out_shape=(jax.ShapeDtypeStruct((8192, 128), F32),) * 2,
        in_specs=[pl.BlockSpec(memory_space=pltpu.VMEM)] * 2,
        out_specs=(pl.BlockSpec(memory_space=pl.ANY),) * 2,
        scratch_shapes=[
            pltpu.VMEM((16, 512, 128), F32),
            pltpu.VMEM((16, 512, 128), F32),
            dma((2, 16)),
        ],
        compiler_params=pltpu.CompilerParams(vmem_limit_bytes=24 * 2**20),
        name="product",
    )(gathered, terms)


def solution(mesh):
    in_specs = (
        P("dp", "tensor"),
        P(("dp", "tensor"), None),
        P(("dp", "tensor"), None),
        P(("dp", "tensor"), None),
        P(("dp", "tensor"), None),
        P(None, ("dp", "tensor")),
    )
    out_specs = (P(None, ("dp", "tensor")), P(None, ("dp", "tensor")))
    return jax.shard_map(local, mesh=mesh, in_specs=in_specs, out_specs=out_specs, check_vma=False)
```

```python
import jax
import jax.numpy as jnp
from jax import lax
from jax.experimental import pallas as pl
from jax.experimental.pallas import tpu as pltpu
from jax.sharding import PartitionSpec as P

epsilon = 1e-05
MESH = pl.DeviceIdType.MESH
BF16, F32 = jnp.bfloat16, jnp.float32
PLANE = (
    (1, 0), (0, 1), (3, 0), (0, 3), (2, 0), (0, 2), (1, 1), (3, 3),
    (1, 3), (3, 1), (1, 2), (2, 1), (3, 2), (2, 3), (2, 2),
)
WAVES = (
    ((0, 2), (1, 2), (2, 2), (3, 2)),
    ((0, 1), (1, 1), (0, 3), (1, 3)),
    ((2, 1), (3, 1), (2, 3), (3, 3)),
    ((0, 0), (1, 0), (2, 0), (3, 0)),
)


def place():
    dp, t = lax.axis_index("dp"), lax.axis_index("tensor")
    return dp // 2, t // 4, ((t // 2) % 2) * 2 + dp % 2, t % 2


def device(x, y, z, c):
    return (x * 2 + z % 2, (y * 2 + z // 2) * 2 + c)


def chip_in_plane(y, z):
    return (z % 2) * 8 + y * 2 + z // 2


def hidden_terms(forward, adjoint):
    gate_pre, up_pre = forward[:, :128], forward[:, 128:256]
    gate_dot, up_dot = forward[:, 256:384], forward[:, 384:]
    cotangent = adjoint.astype(F32)
    logistic = jax.nn.sigmoid(gate_pre)
    first = logistic * (1.0 + gate_pre * (1.0 - logistic))
    second = logistic * (1.0 - logistic) * (2.0 + gate_pre * (1.0 - 2.0 * logistic))
    gate_term = (cotangent * (up_dot * first + up_pre * second * gate_dot)).astype(BF16)
    up_term = (cotangent * first * gate_dot).astype(BF16)
    return gate_term, up_term


def exchange(
    tokens, adjoint, w0, w1, w2, w3, gathered, terms,
    held_tokens, held_adjoint, staged, theirs, packed, arrived, stats, scales, slab, sums, held, sent, passing, part, got,
    load_sem, stage_sem, their_send, their_recv, wave_send, wave_recv, stat_sem, scale_sem,
    a_send, a_recv, b_send, b_recv, x_send, x_left, x_right, f_send, f_left, f_right, d_send, d_recv,
    pass_send, pass_recv, p_send, p_recv,
):
    weights = (w0, w1, w2, w3)
    x, y, z, c = place()
    me = chip_in_plane(y, z)
    right, left, across = (x + 1) % 4, (x + 3) % 4, (x + 2) % 4
    partner = device(x, y, z, 1 - c)
    to_right, to_left = device(right, y, z, c), device(left, y, z, c)
    a, b = y * (1 - c) + z * c, z * (1 - c) + y * c

    def at_ab(to_a, to_b):
        return device(x, to_a * (1 - c) + to_b * c, to_b * (1 - c) + to_a * c, c)

    def stage_copies(w):
        copies = []
        for slot, (m, owner) in enumerate(WAVES[w]):
            start = pl.multiple_of(((x + owner) % 4) * 4096, 4096)
            copies.append(
                pltpu.make_async_copy(
                    weights[m].at[:, pl.ds(start, 4096)],
                    staged.at[w % 2, slot],
                    stage_sem.at[w % 2, slot],
                )
            )
        return copies

    def stage(w):
        for copy in stage_copies(w):
            copy.start()

    def their_copy(w):
        return pltpu.make_async_remote_copy(
            theirs.at[w % 2],
            packed.at[w, :, :, pl.ds(pl.multiple_of(c * 64, 64), 64), :],
            their_send.at[w % 2],
            their_recv.at[w],
            partner,
            MESH,
        )

    def pack(w):
        for copy in stage_copies(w):
            copy.wait()
        if w >= 2:
            their_copy(w - 2).wait_send()

        @pl.loop(0, 16)
        def _(q):
            for m in range(4):
                both = staged[w % 2, m, :, pl.ds(pl.multiple_of(q * 256, 256), 256)]
                low, high = both[:, :128], both[:, 128:]
                packed[w, q, m, pl.ds(pl.multiple_of(c * 64, 64), 64), :] = jnp.where(c == 0, low, high)
                theirs[w % 2, q, m] = jnp.where(c == 0, high, low)

        if w + 2 < 4:
            stage(w + 2)

    def send_wave(w, slots=(0, 4), sem=None):
        slots, sem = pl.ds(slots[0], slots[1]), w if sem is None else sem
        if sem == w:
            their_copy(w).wait_recv()
        for dy, dz in PLANE:
            to_y = (y + dy * (1 - c) + (4 - dz) * c) % 4
            to_z = (z + dz * (1 - c) + (4 - dy) * c) % 4
            pltpu.make_async_remote_copy(
                packed.at[w, chip_in_plane(to_y, to_z), slots],
                arrived.at[w, me, slots],
                wave_send.at[w],
                wave_recv.at[sem],
                device(x, to_y, to_z, c),
                MESH,
            ).start()
        pltpu.make_async_copy(
            packed.at[w, me, slots], arrived.at[w, me, slots], wave_recv.at[sem]
        ).start()

    def wait_bytes(ref, sem):
        pltpu.make_async_copy(ref, ref, sem).wait()

    def share(block, r):
        pltpu.make_async_remote_copy(block, block, d_send, d_recv.at[r], partner, MESH).start()

    column_b = [b, (b + 3) % 4, (b + 1) % 4, (b + 2) % 4]

    def send_x(i, block):
        pltpu.make_async_remote_copy(block, block, x_send, x_left.at[i], to_right, MESH).start()
        pltpu.make_async_remote_copy(block, block, x_send, x_right.at[i], to_left, MESH).start()

    block_a = [a, (a + 3) % 4, (a + 1) % 4, (a + 2) % 4]

    def send_block(k):
        block = gathered.at[x, block_a[k], c, b]
        if k > 0:
            wait_bytes(block, a_recv.at[k - 1])
        for i, d in enumerate((1, 3, 2)):
            pltpu.make_async_remote_copy(
                block, block, b_send, b_recv.at[i, k], at_ab(a, (b + d) % 4), MESH
            ).start()
        send_x(0, block)

    def relay_block(i, k):
        block = gathered.at[x, block_a[k], c, column_b[i]]
        wait_bytes(block, b_recv.at[i - 1, k])
        send_x(i, block)

    def normalise(from_x):
        @pl.loop(0, 16)
        def _(i):
            at_a, at_b = i // 4, i % 4
            for from_c in range(2):
                from_z = at_a if from_c else at_b
                scale = scales[from_x * 2 + from_z % 2][:1]
                block = gathered[from_x, at_a, from_c, at_b].astype(F32)
                gathered[from_x, at_a, from_c, at_b] = (block * scale).astype(BF16)

    def pass_on(i):
        block = gathered.at[left, :, c, column_b[i]]
        wait_bytes(block, x_left.at[i])
        half = gathered.at[left, pl.ds(0, 2), c, column_b[i]]
        pltpu.make_async_remote_copy(half, half, f_send, f_left.at[i], to_right, MESH).start()
        share(block, 1)
        block = gathered.at[right, :, c, column_b[i]]
        wait_bytes(block, x_right.at[i])
        half = gathered.at[right, pl.ds(2, 2), c, column_b[i]]
        pltpu.make_async_remote_copy(half, half, f_send, f_right.at[i], to_left, MESH).start()
        share(block, 2)

    def take_across(i):
        wait_bytes(gathered.at[across, pl.ds(0, 2), c, column_b[i]], f_left.at[i])
        wait_bytes(gathered.at[across, pl.ds(2, 2), c, column_b[i]], f_right.at[i])
        share(gathered.at[across, :, c, column_b[i]], 3)

    def forward(w, rows, slots=range(4)):
        lhs = jnp.concatenate([slab[k, rows, :] for k in range(4)], axis=1)
        rhs = jnp.concatenate([arrived[w, :, m].reshape(2048, 128) for m in slots], axis=1)
        return jnp.dot(lhs, rhs, preferred_element_type=F32)

    def quarter(q):
        return pl.ds(pl.multiple_of(q * 256, 256), 256)

    def x_neighbour(way):
        return device((x + 1 + 2 * way) % 4, y, z, c)

    def make_slab(q, r):
        wait_bytes(gathered.at[q, :, 1 - c], d_recv.at[r])
        for from_z in range(4):
            for from_c in range(2):
                rows = pl.ds(pl.multiple_of(q * 256 + from_z % 2 * 128, 128), 128)
                scale = scales[q * 2 + from_z % 2][:1]
                block = gathered[q, from_z, 1, x] if from_c else gathered[q, x, 0, from_z]
                block = (block.astype(F32) * scale).astype(BF16)
                slab[(from_z // 2) * 2 + from_c, rows, :] = jnp.transpose(block)

    def pass_copy(q):
        return pltpu.make_async_remote_copy(
            sent.at[q], passing.at[q], pass_send.at[q], pass_recv.at[q], x_neighbour(q // 2), MESH
        )

    def forward_across(q):
        sent[q] = forward(0, quarter(q)).astype(BF16)
        pass_copy(q).start()

    def part_copy(w, q, late, way):
        pltpu.make_async_remote_copy(
            part.at[w - 1, late, q], got.at[w - 1, way, q], p_send, p_recv.at[q], x_neighbour(way), MESH
        ).start()

    def forward_beside(w, q):
        total = forward(w, quarter(q))
        to_r, to_l = total[:, :256], total[:, 256:]
        way = q // 2
        part[w - 1, 0, q] = jnp.where(way == 0, to_l, to_r).astype(BF16)
        part_copy(w, q, 0, 1 - way)
        held[w - 1, q] = jnp.where(way == 0, to_r, to_l)

    def add_passing(w, q):
        add = passing[q, :, (w - 1) * 256 : w * 256].astype(F32)
        part[w - 1, 1, q] = (held[w - 1, q] + add).astype(BF16)
        part_copy(w, q, 1, q // 2)

    barrier = pltpu.get_barrier_semaphore()
    peers = [device(x, (y + dy) % 4, (z + dz) % 4, c) for dy, dz in PLANE]
    stat_peers = [
        device(x, (y + dy) % 4, (z + dz) % 4, (c + dc) % 2)
        for dy in range(4) for dz in (0, 2) for dc in range(2) if dy or dz or dc
    ]
    cross_peers = [
        device(x, (y + dy) % 4, (z + dz) % 4, 1 - c) for dy in range(4) for dz in (0, 2)
    ]
    flipped = z + 1 - 2 * (z % 2)
    dp_peers = [device((x + dx) % 4, y, flipped, c) for dx in (1, 2, 3)]
    x_peers = [device((x + dx) % 4, y, z, c) for dx in (1, 2, 3)]
    everyone = peers + cross_peers + x_peers + dp_peers
    for peer in everyone:
        pl.semaphore_signal(barrier, 1, device_id=peer, device_id_type=MESH)

    load_tokens = pltpu.make_async_copy(tokens, held_tokens, load_sem.at[0])
    load_tokens.start()
    load_adjoint = pltpu.make_async_copy(adjoint, held_adjoint, load_sem.at[1])
    load_adjoint.start()
    stage(0)
    stage(1)
    load_tokens.wait()
    turned = jnp.transpose(held_tokens[...])
    mine = gathered.at[x, a, c, b]
    mine[...] = turned
    pl.semaphore_wait(barrier, len(everyone))
    for i, d in enumerate((1, 3, 2)):
        pltpu.make_async_remote_copy(
            mine, mine, a_send, a_recv.at[i], at_ab((a + d) % 4, b), MESH
        ).start()
    send_block(0)
    send_block(1)
    send_block(2)
    pack(0)
    their_copy(0).start()
    relay_block(1, 0)
    relay_block(2, 0)
    send_block(3)
    relay_block(3, 0)
    share(gathered.at[x, :, c, b], 0)
    send_wave(0)
    wide = turned.astype(F32)
    t = lax.axis_index("tensor")
    stats[t] = jnp.broadcast_to(jnp.sum(wide * wide, axis=0, keepdims=True), (8, 128))
    for peer in stat_peers:
        pltpu.make_async_remote_copy(
            stats.at[t], stats.at[t], stat_sem.at[0], stat_sem.at[1], peer, MESH
        ).start()
    pack(1)
    their_copy(1).start()
    for k in (1, 2, 3):
        for i in (1, 2, 3):
            relay_block(i, k)
    for i in (1, 2, 3):
        share(gathered.at[x, :, c, column_b[i]], 0)
    send_wave(1)
    pack(2)
    their_copy(2).start()
    wait_bytes(stats.at[pl.ds(0, 15)], stat_sem.at[1])
    total = stats[0]
    for i in range(1, 16):
        total = total + stats[i]
    dp = lax.axis_index("dp")
    scales[dp] = lax.rsqrt(total * (1.0 / 8192.0) + epsilon)
    for peer in x_peers + dp_peers + [device(x, y, flipped, c)]:
        pltpu.make_async_remote_copy(
            scales.at[dp], scales.at[dp], scale_sem.at[0], scale_sem.at[1], peer, MESH
        ).start()
    pass_on(0)
    send_wave(2)
    pack(3)
    their_copy(3).start()
    pass_on(1)
    take_across(0)
    send_wave(3, (0, 2))
    send_wave(3, (2, 2), 4)
    wait_bytes(scales.at[pl.ds(0, 7)], scale_sem.at[1])
    make_slab(x, 0)
    wait_bytes(arrived.at[0], wave_recv.at[0])
    forward_across(x)
    pass_on(2)
    take_across(1)
    pass_on(3)
    make_slab(left, 1)
    forward_across(left)
    make_slab(right, 2)
    forward_across(right)
    take_across(2)
    take_across(3)
    wait_bytes(arrived.at[1], wave_recv.at[1])
    forward_beside(1, x)
    forward_beside(1, left)
    forward_beside(1, right)
    make_slab(across, 3)
    forward_across(across)
    forward_beside(1, across)
    @pl.loop(0, 4)
    def _(q):
        pass_copy(q).wait_recv()
        add_passing(1, q)

    wait_bytes(arrived.at[2], wave_recv.at[2])

    @pl.loop(0, 4)
    def _(q):
        forward_beside(2, q)
        add_passing(2, q)

    wait_bytes(gathered.at[0, 0, 0, pl.ds(0, 3)], a_send)
    wait_bytes(gathered.at[0, pl.ds(0, 3), 0], b_send)
    wait_bytes(gathered.at[0], x_send)
    wait_bytes(gathered.at[0, pl.ds(0, 2)], f_send)
    wait_bytes(gathered.at[pl.ds(0, 2)], d_send)

    @pl.loop(0, 4)
    def _(q):
        normalise(q)

    for pair in range(2):
        wait_bytes(arrived.at[3, :, pl.ds(pair * 2, 2)], wave_recv.at[3 + pair])
        for half in range(2):
            rows = pl.ds(half * 512, 512)
            sums[rows, pair * 256 : pair * 256 + 256] = forward(3, rows, (pair * 2, pair * 2 + 1))

    load_adjoint.wait()

    @pl.loop(0, 4)
    def _(q):
        wait_bytes(got.at[0, :, pl.ds(0, 2)], p_recv.at[q])
        total = sums[quarter(q), :]
        for way in range(2):
            total = total + jnp.concatenate([got[0, way, q], got[1, way, q]], axis=1).astype(F32)
        gate_term, up_term = hidden_terms(total, held_adjoint[quarter(q), :])
        terms[quarter(q), :128] = gate_term
        terms[quarter(q), 128:] = up_term

    for q in range(4):
        pass_copy(q).wait_send()
    wait_bytes(part, p_send)
    for w in range(4):
        wait_bytes(packed.at[w, pl.ds(0, 15)], wave_send.at[w])
    for w in (2, 3):
        their_copy(w).wait_send()
    wait_bytes(stats.at[pl.ds(0, 15)], stat_sem.at[0])
    wait_bytes(scales.at[pl.ds(0, 7)], scale_sem.at[0])


def product(gathered, terms, gate, up, gate_out, up_out, out_sem):
    def stores(t):
        rows = pl.ds(512 * t, 512)
        return (
            pltpu.make_async_copy(gate_out.at[t], gate.at[rows], out_sem.at[0, t]),
            pltpu.make_async_copy(up_out.at[t], up.at[rows], out_sem.at[1, t]),
        )

    for t in range(16):
        row, pair = t // 4, ((t // 2) % 2) * 2
        lhs = jnp.concatenate(
            [
                gathered[i, row, 0, pair + j] if t % 2 == 0 else gathered[i, pair + j, 1, row]
                for i in range(4)
                for j in range(2)
            ],
            axis=1,
        )
        result = jnp.dot(lhs, terms[...], preferred_element_type=F32)
        gate_out[t] = result[:, :128]
        up_out[t] = result[:, 128:]
        for store in stores(t):
            store.start()
    for t in range(16):
        for store in stores(t):
            store.wait()


def local(tokens, gate_weight, up_weight, gate_tangent, up_tangent, adjoint):
    dma = pltpu.SemaphoreType.DMA
    gathered, terms = pl.pallas_call(
        exchange,
        out_shape=(
            pltpu.VMEM((4, 4, 2, 4, 512, 128), BF16),
            pltpu.VMEM((1024, 256), BF16),
        ),
        in_specs=[pl.BlockSpec(memory_space=pl.ANY)] * 6,
        out_specs=(pl.BlockSpec(memory_space=pltpu.VMEM),) * 2,
        scratch_shapes=[
            pltpu.VMEM((128, 512), BF16),
            pltpu.VMEM((1024, 128), BF16),
            pltpu.VMEM((2, 4, 64, 4096), BF16),
            pltpu.VMEM((2, 16, 4, 64, 128), BF16),
            pltpu.VMEM((4, 16, 4, 128, 128), BF16),
            pltpu.VMEM((4, 16, 4, 128, 128), BF16),
            pltpu.VMEM((16, 8, 128), F32),
            pltpu.VMEM((8, 8, 128), F32),
            pltpu.VMEM((4, 1024, 512), BF16),
            pltpu.VMEM((1024, 512), F32),
            pltpu.VMEM((2, 4, 256, 256), F32),
            pltpu.VMEM((4, 256, 512), BF16),
            pltpu.VMEM((4, 256, 512), BF16),
            pltpu.VMEM((2, 2, 4, 256, 256), BF16),
            pltpu.VMEM((2, 2, 4, 256, 256), BF16),
            dma((2,)), dma((2, 4)), dma((2,)), dma((4,)), dma((4,)), dma((5,)), dma((2,)), dma((2,)),
            dma, dma((3,)), dma, dma((3, 4)), dma, dma((4,)), dma((4,)), dma, dma((4,)), dma((4,)), dma, dma((4,)),
            dma((4,)), dma((4,)), dma, dma((4,)),
        ],
        compiler_params=pltpu.CompilerParams(
            collective_id=0, has_side_effects=True, vmem_limit_bytes=44 * 2**20
        ),
        name="exchange",
    )(tokens, adjoint, gate_weight, up_weight, gate_tangent, up_tangent)

    gathered = pltpu.with_memory_space_constraint(gathered, pltpu.VMEM)
    terms = pltpu.with_memory_space_constraint(terms, pltpu.VMEM)
    return pl.pallas_call(
        product,
        out_shape=(jax.ShapeDtypeStruct((8192, 128), F32),) * 2,
        in_specs=[pl.BlockSpec(memory_space=pltpu.VMEM)] * 2,
        out_specs=(pl.BlockSpec(memory_space=pl.ANY),) * 2,
        scratch_shapes=[
            pltpu.VMEM((16, 512, 128), F32),
            pltpu.VMEM((16, 512, 128), F32),
            dma((2, 16)),
        ],
        compiler_params=pltpu.CompilerParams(vmem_limit_bytes=24 * 2**20),
        name="product",
    )(gathered, terms)


def solution(mesh):
    in_specs = (
        P("dp", "tensor"),
        P(("dp", "tensor"), None),
        P(("dp", "tensor"), None),
        P(("dp", "tensor"), None),
        P(("dp", "tensor"), None),
        P(None, ("dp", "tensor")),
    )
    out_specs = (P(None, ("dp", "tensor")), P(None, ("dp", "tensor")))
    return jax.shard_map(local, mesh=mesh, in_specs=in_specs, out_specs=out_specs, check_vma=False)
```
